128 devices in a mesh: context: 32 (over z, x, core), tensor: 4 (over y).
Axes of the slice: x: 4, y: 4, z: 4, core: 2. Of those that a mesh axis runs over, the one named last changes fastest.
Arguments:
- query_in: bfloat16 [2, 4096, 4096], P(None, 'context', 'tensor'), may hold values from -6 to 6
- key_in: bfloat16 [2, 4096, 4096], P(None, 'context', 'tensor'), may hold values from -6 to 6
- value_in: bfloat16 [2, 4096, 4096], P(None, 'context', 'tensor'), may hold values from -6 to 6
- short_filter: float32 [3, 7, 256], P(None, None, 'tensor'), may hold values from -2.4 to 2.4
- long_filter: float32 [256, 4096], P(('tensor', 'context')), may hold values from 0 to 1
- out_weight: bfloat16 [4096, 4096], P('context', 'tensor'), may hold values from -0.09375 to 0.09375
- grad_out: bfloat16 [2, 4096, 4096], P(None, 'context', 'tensor'), may hold values from -6 to 6
Outputs:
- mixed_out: bfloat16 [2, 4096, 4096], P(None, 'context', 'tensor')
- grad_query: bfloat16 [2, 4096, 4096], P(None, 'context', 'tensor')
- grad_key: bfloat16 [2, 4096, 4096], P(None, 'context', 'tensor')
- grad_value: bfloat16 [2, 4096, 4096], P(None, 'context', 'tensor')
- grad_weight: float32 [4096, 4096], P('context', 'tensor')
- grad_long: float32 [256, 4096], P(('tensor', 'context'))
The draws below stay inside these ranges and needn't reach their ends.
All inputs are finite; a program needn't handle non-finite values.
Results may differ from the reference program's by a relative error of at most 0.015.
Values may be sent and summed in bfloat16 or wider, within the bound.
No kernel may reach another device: no remote copies, remote signals or barrier semaphores. Data moves between devices by JAX's collectives and lax.ppermute only.
A program may use at most 128 MiB of HBM per device.

```python
import math
import jax
import jax.numpy as jnp
from jax import lax

CH = 4096
OUT = 4096
GROUP = 16
TAPS = 7
SEQS = 2
SEQUENCE_LENGTH = 4096
FILTER_GROUPS = 256


def draw_long_filter(key, part):
    random_child_keys = jax.random.split(key, 6)
    sequence_offset = jnp.arange(SEQUENCE_LENGTH, dtype=jnp.float32)[None, :]
    slow_share = 0.5
    rough_low = 0.5
    rough_high = 1.5
    is_slow = jax.random.bernoulli(random_child_keys[0], slow_share, (FILTER_GROUPS, 1))
    slow_rate = jnp.exp(jax.random.uniform(random_child_keys[1], (FILTER_GROUPS, 1), jnp.float32, math.log(0.1 / SEQUENCE_LENGTH), math.log(0.8 / SEQUENCE_LENGTH)))
    fast_rate = jnp.exp(jax.random.uniform(random_child_keys[2], (FILTER_GROUPS, 1), jnp.float32, math.log(1.0 / 50.0), math.log(1.0 / 30.0)))
    falloff_speed = jnp.where(is_slow, slow_rate, fast_rate)
    filter_jitter = jax.random.uniform(random_child_keys[3], (FILTER_GROUPS, SEQUENCE_LENGTH), jnp.float32, rough_low, rough_high)
    spike_position = jax.random.randint(random_child_keys[4], (FILTER_GROUPS, 2), 0, SEQUENCE_LENGTH)
    spike_retained = jax.random.uniform(random_child_keys[5], (FILTER_GROUPS, 2), jnp.float32, 0.5, 0.8)
    spike_values = jnp.where(sequence_offset >= spike_position[:, 0:1].astype(jnp.float32), spike_retained[:, 0:1], 1.0)
    spike_values = spike_values * jnp.where(sequence_offset >= spike_position[:, 1:2].astype(jnp.float32), spike_retained[:, 1:2], 1.0)
    signal_power = jnp.expm1(-2.0 * falloff_speed * SEQUENCE_LENGTH) / jnp.expm1(-2.0 * falloff_speed)
    filter_samples = filter_jitter * spike_values * jnp.exp(-falloff_speed * sequence_offset) / jnp.sqrt(signal_power)
    return filter_samples.astype(jnp.float32)


def raised(entries, rng, source, target, parts, factor):
    def block_of(axis_at):
        return (jnp.arange(entries.shape[axis_at]) // (entries.shape[axis_at] // parts)).reshape((-1,) + (1,) * (entries.ndim - 1 - axis_at))

    near = jax.random.permutation(rng, parts)[block_of(target)]
    second = (block_of(target) + parts // 2) % parts
    return jnp.where((block_of(source) == near) | (block_of(source) == second), factor * entries, entries)


def levels(rng, extent, cuts, least, largest):
    factor_of, own = 1.0, jax.random.fold_in(rng, 6)
    for position, blocks in cuts:
        heights = jnp.exp(jax.random.uniform(jax.random.fold_in(own, position), (blocks,), jnp.float32, least / len(cuts), largest / len(cuts)))
        factor_of = factor_of * jnp.repeat(heights, extent[position] // blocks).reshape([-1 if axis == position else 1 for axis in range(len(extent))])
    return factor_of


def normal_values(rng, shape, width, reach, shards=(), kind=jnp.bfloat16):
    array = jax.random.normal(rng, shape, jnp.float32) * width
    if len(shards) > 0:
        array = levels(rng, shape, shards, -0.22, 0.18) * array
    return jnp.clip(array, min=-reach, max=reach).astype(kind)


def noise_with(rng, dims, deviation, most, cuts, heavy, held_as=jnp.bfloat16):
    result = deviation * jax.random.normal(rng, dims, jnp.float32)
    if cuts:
        result = result * levels(rng, dims, cuts, -0.22, 0.18)
    return jnp.clip(raised(result, jax.random.fold_in(rng, 3), *heavy), -most, most).astype(held_as)


def setup_inputs(seed: int = 0) -> dict:
    keys = jax.random.split(jax.random.key(seed), 8)
    return {
        "query_in": normal_values(keys[0], (SEQS, SEQUENCE_LENGTH, CH), 1.0, 6.0, ((1, 32), (2, 4))),
        "key_in": normal_values(keys[1], (SEQS, SEQUENCE_LENGTH, CH), 1.0, 6.0, ((1, 32), (2, 4))),
        "value_in": normal_values(keys[2], (SEQS, SEQUENCE_LENGTH, CH), 1.0, 6.0, ((1, 32), (2, 4))),
        "short_filter": normal_values(keys[3], (3, TAPS, FILTER_GROUPS), 0.4, 2.4, ((2, 4),), jnp.float32),
        "long_filter": draw_long_filter(jax.random.fold_in(keys[7], 71), 0),
        "out_weight": normal_values(keys[5], (OUT, CH), CH ** -0.5, 0.09375, ((0, 32), (1, 4))),
        "grad_out": noise_with(keys[6], (SEQS, SEQUENCE_LENGTH, OUT), 1.0, 6.0, ((1, 32), (2, 4)), (1, 2, 32, 2.75)),
    }


chan_block = 256


def featurize(signal, tap_weights):
    length = signal.shape[1]
    padded = jnp.pad(signal.astype(jnp.float32), ((0, 0), (TAPS - 1, 0), (0, 0)))
    summed = jnp.zeros(signal.shape, jnp.float32)
    for offset in range(TAPS):
        lead_at = TAPS - 1 - offset
        summed = summed + tap_weights[offset] * padded[:, lead_at:lead_at + length]
    return summed


def unfeaturize(gradient, tap_weights):
    length = gradient.shape[1]
    padded = jnp.pad(gradient, ((0, 0), (0, TAPS - 1), (0, 0)))
    summed = jnp.zeros(gradient.shape, jnp.float32)
    for offset in range(TAPS):
        summed = summed + tap_weights[offset] * padded[:, offset:offset + length]
    return summed


def reference(query_in, key_in, value_in, short_filter, long_filter, out_weight, grad_out):
    transform_len = 2 * SEQUENCE_LENGTH
    grad_scale = float(SEQS * SEQUENCE_LENGTH * GROUP) ** -0.5
    grad_full = grad_out.astype(jnp.float32)
    group_block = chan_block // GROUP
    block_count = CH // chan_block

    def one_block(mixed_sum, block_index):
        chan_start = block_index * chan_block
        group_start = block_index * group_block
        query_block = lax.dynamic_slice_in_dim(query_in, chan_start, chan_block, 2)
        key_block = lax.dynamic_slice_in_dim(key_in, chan_start, chan_block, 2)
        value_block = lax.dynamic_slice_in_dim(value_in, chan_start, chan_block, 2)
        tap_weights = jnp.repeat(lax.dynamic_slice_in_dim(short_filter, group_start, group_block, 2), GROUP, axis=2).astype(jnp.float32)
        query_feat = featurize(query_block, tap_weights[0])
        key_feat = featurize(key_block, tap_weights[1])
        value_feat = featurize(value_block, tap_weights[2])
        product = (key_feat * value_feat).astype(jnp.bfloat16)
        kernel = lax.dynamic_slice_in_dim(long_filter, group_start, group_block, 0).astype(jnp.float32)
        kernel_spec = jnp.repeat(jnp.fft.rfft(kernel, n=transform_len, axis=1), GROUP, axis=0).T
        product_spec = jnp.fft.rfft(product.astype(jnp.float32), n=transform_len, axis=1)
        conv_out = jnp.fft.irfft(product_spec * kernel_spec, n=transform_len, axis=1)[:, :SEQUENCE_LENGTH].astype(jnp.bfloat16)
        gated = (query_feat * conv_out.astype(jnp.float32)).astype(jnp.bfloat16)
        weight_block = lax.dynamic_slice_in_dim(out_weight, chan_start, chan_block, 1).astype(jnp.float32)
        mixed_sum = mixed_sum + jnp.einsum('blc,oc->blo', gated.astype(jnp.float32), weight_block)
        grad_gated = jnp.einsum('blo,oc->blc', grad_full, weight_block)
        grad_conv = (grad_gated * query_feat).astype(jnp.bfloat16)
        grad_weight = jnp.einsum('blo,blc->oc', grad_full, gated.astype(jnp.float32))
        conv_spec = jnp.fft.rfft(grad_conv.astype(jnp.float32), n=transform_len, axis=1)
        grad_product = jnp.fft.irfft(conv_spec * jnp.conj(kernel_spec), n=transform_len, axis=1)[:, :SEQUENCE_LENGTH].astype(jnp.bfloat16)
        crossed = jnp.sum(conv_spec * jnp.conj(product_spec), axis=0)
        crossed = jnp.sum(crossed.reshape(SEQUENCE_LENGTH + 1, group_block, GROUP), axis=2)
        grad_long = jnp.fft.irfft(crossed, n=transform_len, axis=0)[:SEQUENCE_LENGTH].T * grad_scale
        grad_qfeat = grad_gated * conv_out.astype(jnp.float32)
        grad_kfeat = grad_product.astype(jnp.float32) * value_feat
        grad_vfeat = grad_product.astype(jnp.float32) * key_feat
        grad_query = unfeaturize(grad_qfeat, tap_weights[0]).astype(jnp.bfloat16)
        grad_key = unfeaturize(grad_kfeat, tap_weights[1]).astype(jnp.bfloat16)
        grad_value = unfeaturize(grad_vfeat, tap_weights[2]).astype(jnp.bfloat16)
        return mixed_sum, (grad_query, grad_key, grad_value, grad_weight, grad_long)

    mixed_sum, stacked = lax.scan(one_block, jnp.zeros((SEQS, SEQUENCE_LENGTH, OUT), jnp.float32), jnp.arange(block_count, dtype=jnp.int32))
    grad_query = jnp.moveaxis(stacked[0], 0, 2).reshape(SEQS, SEQUENCE_LENGTH, CH)
    grad_key = jnp.moveaxis(stacked[1], 0, 2).reshape(SEQS, SEQUENCE_LENGTH, CH)
    grad_value = jnp.moveaxis(stacked[2], 0, 2).reshape(SEQS, SEQUENCE_LENGTH, CH)
    grad_weight = jnp.moveaxis(stacked[3], 0, 1).reshape(OUT, CH)
    grad_long = stacked[4].reshape(FILTER_GROUPS, SEQUENCE_LENGTH)
    return (mixed_sum.astype(jnp.bfloat16), grad_query, grad_key, grad_value, grad_weight, grad_long)
```

```python
import functools

import jax
import jax.numpy as jnp
from jax import lax
from jax.experimental import pallas as pl
from jax.experimental.pallas import tpu as pltpu
from jax.sharding import PartitionSpec as P

GROUP = 16
TAPS = 7
HALO = 16
NZ, NX, NC, NY = 4, 4, 2, 4
NCTX = NZ * NX * NC
BLK = 128
CB = 256
f32 = jnp.float32
bf16 = jnp.bfloat16


def move_ctx(value, dz, dx, dc):
    pairs = []
    for z in range(NZ):
        for x in range(NX):
            for c in range(NC):
                src = (z * NX + x) * NC + c
                dst = (((z + dz) % NZ) * NX + (x + dx) % NX) * NC + (c + dc) % NC
                pairs.append((src, dst))
    return lax.ppermute(value, "context", pairs)


def move_z(value, d):
    return move_ctx(value, d, 0, 0)


def move_x(value, d):
    return move_ctx(value, 0, d, 0)


def swap_core(value):
    return move_ctx(value, 0, 0, 1)


def move_y(value, d):
    return lax.ppermute(value, "tensor", [(i, (i + d) % NY) for i in range(NY)])


def next_context(value, steps):
    first, last = (max(0, -steps), min(NCTX, NCTX - steps))
    return lax.ppermute(value, "context", [(s, s + steps) for s in range(first, last)])


def around(value, move, count=4):
    return [value] + [move(value, d) for d in range(1, count)]


def deliver(parts, move):
    return [parts[0]] + [move(part, d) for d, part in enumerate(parts) if d > 0]


def params(*sem):
    return pltpu.CompilerParams(dimension_semantics=sem, vmem_limit_bytes=48 * 1024 * 1024)


def toeplitz_kernel(filter_ref, tile_ref):
    taps = jnp.concatenate([jnp.zeros((1, BLK), f32), filter_ref[0]], axis=1)
    blocks = taps.shape[1] // BLK - 1
    tile_ref[0, 0, BLK:, :BLK] = jnp.zeros((BLK, BLK), bf16)
    for e in range(blocks):
        window = jnp.broadcast_to(taps[:, BLK * e : BLK * (e + 2)], (BLK, 2 * BLK))
        rolled = pltpu.roll(window, 0, 1, stride=1, stride_axis=0)
        piece = rolled[:, BLK:].astype(bf16)
        if e % 2 == 0:
            tile_ref[0, e // 2, :BLK, :BLK] = piece
            tile_ref[0, e // 2, BLK:, BLK:] = piece
        else:
            tile_ref[0, e // 2, :BLK, BLK:] = piece
            if e + 1 < blocks:
                tile_ref[0, e // 2 + 1, BLK:, :BLK] = piece


def toeplitz_tiles(long_filter):
    groups, length = long_filter.shape
    tiles = length // (2 * BLK)
    return pl.pallas_call(
        toeplitz_kernel,
        grid=(groups,),
        in_specs=[pl.BlockSpec((1, 1, length), lambda g: (g, 0, 0))],
        out_specs=pl.BlockSpec((1, tiles, 2 * BLK, 2 * BLK), lambda g: (g, 0, 0, 0)),
        out_shape=jax.ShapeDtypeStruct((groups, tiles, 2 * BLK, 2 * BLK), bf16),
        compiler_params=params("arbitrary"),
        cost_estimate=pl.CostEstimate(flops=8_000_000, bytes_accessed=4_300_000, transcendentals=0),
        name="toeplitz_tiles",
    )(long_filter[:, None, :])


def spread_taps(taps, block):
    rows = lax.broadcasted_iota(jnp.int32, (taps.shape[1], CB), 0)
    cols = lax.broadcasted_iota(jnp.int32, (taps.shape[1], CB), 1)
    spread = (rows == ((block * CB + cols) >> 4)).astype(f32)
    return jnp.dot(taps, spread, precision=lax.Precision.HIGHEST, preferred_element_type=f32)


def to_channels(value):
    return value.T.reshape(CB // (2 * GROUP), 2, GROUP, BLK).astype(bf16)


def to_positions(value):
    return value.astype(f32).reshape(CB, BLK).T


def featurize_kernel(taps_ref, halo_ref, q_ref, k_ref, v_ref, prod_ref, qf_ref, kf_ref, vf_ref):
    taps = spread_taps(taps_ref[...], pl.program_id(0))
    for b in range(2):
        feats = []
        for i, (src, dst) in enumerate(((q_ref, qf_ref), (k_ref, kf_ref), (v_ref, vf_ref))):
            ext = jnp.concatenate([halo_ref[i, b].astype(f32), src[b].astype(f32)], axis=0)
            total = taps[7 * i : 7 * i + 1] * ext[HALO:]
            for j in range(1, TAPS):
                total = total + taps[7 * i + j : 7 * i + j + 1] * ext[HALO - j : HALO - j + BLK]
            dst[b] = total
            feats.append(total)
        prod_ref[:, :, b] = to_channels(feats[1] * feats[2])


chan_spec = pl.BlockSpec((CB // (2 * GROUP), 2, 2, GROUP, BLK), lambda c: (c, 0, 0, 0, 0))
pos_spec = pl.BlockSpec((2, BLK, CB), lambda c: (0, 0, c))
taps_spec = pl.BlockSpec((24, 64), lambda c: (0, 0))
halo_spec = pl.BlockSpec((3, 2, HALO, CB), lambda c: (0, 0, 0, c))


def chan_shape():
    return jax.ShapeDtypeStruct((NCTX, 2, 2, GROUP, BLK), bf16)


def pos_shape(kind):
    return jax.ShapeDtypeStruct((2, BLK, 1024), kind)


def featurize(taps, halo, q, k, v):
    return pl.pallas_call(
        featurize_kernel,
        grid=(1024 // CB,),
        in_specs=[taps_spec, halo_spec, pos_spec, pos_spec, pos_spec],
        out_specs=[chan_spec, pos_spec, pos_spec, pos_spec],
        out_shape=[chan_shape(), pos_shape(f32), pos_shape(f32), pos_shape(f32)],
        compiler_params=params("arbitrary"),
        cost_estimate=pl.CostEstimate(flops=12_000_000, bytes_accessed=5_500_000, transcendentals=0),
        name="featurize",
    )(taps, halo, q, k, v)


def fold(src_ref, dst_ref):
    for i in range(NCTX // 2):
        dst_ref[32 * i : 32 * i + 32, :BLK] = src_ref[2 * i, 0].reshape(32, BLK)
        dst_ref[32 * i : 32 * i + 32, BLK:] = src_ref[2 * i + 1, 0].reshape(32, BLK)


def unfold(acc_ref, dst_ref):
    for i in range(NCTX // 2):
        rows = acc_ref[32 * i : 32 * i + 32].astype(bf16)
        dst_ref[2 * i, 0] = rows[:, :BLK].reshape(2, GROUP, BLK)
        dst_ref[2 * i + 1, 0] = rows[:, BLK:].reshape(2, GROUP, BLK)


def conv_kernel(x_ref, tile_ref, out_ref, x_s, acc_s):
    fold(x_ref, x_s)
    rows = x_s.shape[0]
    for d in range(rows // 32):
        term = jnp.dot(x_s[: rows - 32 * d], tile_ref[0, d], preferred_element_type=f32)
        if d == 0:
            acc_s[...] = term
        else:
            acc_s[32 * d :] += term
    unfold(acc_s, out_ref)


def corr_kernel(x_ref, tile_ref, out_ref, x_s, acc_s):
    fold(x_ref, x_s)
    rows = x_s.shape[0]
    for d in range(rows // 32):
        term = lax.dot_general(
            x_s[32 * d :], tile_ref[0, d], (((1,), (1,)), ((), ())), preferred_element_type=f32
        )
        if d == 0:
            acc_s[...] = term
        else:
            acc_s[: rows - 32 * d] += term
    unfold(acc_s, out_ref)


group_spec = pl.BlockSpec((NCTX, 1, 2, GROUP, BLK), lambda g: (0, g, 0, 0, 0))
tile_spec = pl.BlockSpec((1, 16, 2 * BLK, 2 * BLK), lambda g: (g, 0, 0, 0))


def convolve(kernel, name, x, tiles):
    return pl.pallas_call(
        kernel,
        grid=(2,),
        in_specs=[group_spec, tile_spec],
        out_specs=group_spec,
        out_shape=chan_shape(),
        scratch_shapes=[pltpu.VMEM((512, 256), bf16), pltpu.VMEM((512, 256), f32)],
        compiler_params=params("arbitrary"),
        cost_estimate=pl.CostEstimate(flops=1_100_000_000, bytes_accessed=5_300_000, transcendentals=0),
        name=name,
    )(x, tiles)


def grad_long_kernel(scale, p_ref, g_ref, out_ref, p_s, g_s):
    fold(p_ref, p_s)
    fold(g_ref, g_s)
    g_s[512:] = jnp.zeros((512, 256), bf16)
    rows = lax.broadcasted_iota(jnp.int32, (256, 256), 0)
    cols = lax.broadcasted_iota(jnp.int32, (256, 256), 1)
    flip = (rows + cols == 255).astype(bf16)
    back = lax.dot_general(
        flip, p_s[...], (((1,), (1,)), ((), ())), preferred_element_type=f32
    ).astype(bf16)

    def diagonals(block):
        padded = jnp.concatenate([block, jnp.zeros((BLK, BLK), f32)], axis=1)
        rolled = pltpu.roll(padded, 1, 1, stride=1, stride_axis=0)
        return jnp.sum(rolled, axis=0, keepdims=True)

    def gram(d):
        return jnp.dot(back, g_s[32 * d : 32 * d + 512], preferred_element_type=f32)

    here = gram(0)
    lag = diagonals(here[BLK:, :BLK] + here[:BLK, BLK:])
    for d in range(16):
        later = gram(d + 1) if d < 15 else None
        cross = here[BLK:, BLK:]
        if later is not None:
            cross = cross + later[:BLK, :BLK]
        odd = diagonals(cross)
        out_ref[0, :, 256 * d : 256 * d + BLK] = scale * (lag[:, BLK:] + odd[:, :BLK])
        if later is not None:
            lag = diagonals(later[BLK:, :BLK] + later[:BLK, BLK:])
            out_ref[0, :, 256 * d + BLK : 256 * d + 256] = scale * (odd[:, BLK:] + lag[:, :BLK])
        else:
            out_ref[0, :, 256 * d + BLK : 256 * d + 256] = scale * odd[:, BLK:]
        here = later


def grad_long_call(scale, prod, grad_conv):
    return pl.pallas_call(
        functools.partial(grad_long_kernel, scale),
        grid=(2,),
        in_specs=[group_spec, group_spec],
        out_specs=pl.BlockSpec((1, 1, NCTX * BLK), lambda g: (g, 0, 0)),
        out_shape=jax.ShapeDtypeStruct((2, 1, NCTX * BLK), f32),
        scratch_shapes=[pltpu.VMEM((512, 256), bf16), pltpu.VMEM((1024, 256), bf16)],
        compiler_params=params("arbitrary"),
        cost_estimate=pl.CostEstimate(flops=2_200_000_000, bytes_accessed=1_200_000, transcendentals=0),
        name="grad_long",
    )(prod, grad_conv)[:, 0]


def gate_kernel(conv_ref, qf_ref, gated_ref, convp_ref):
    for b in range(2):
        conv = to_positions(conv_ref[:, :, b])
        convp_ref[b] = conv.astype(bf16)
        gated_ref[b] = (qf_ref[b] * conv).astype(bf16)


def gate(conv, qf):
    return pl.pallas_call(
        gate_kernel,
        grid=(1024 // CB,),
        in_specs=[chan_spec, pos_spec],
        out_specs=[pos_spec, pos_spec],
        out_shape=[pos_shape(bf16), pos_shape(bf16)],
        compiler_params=params("arbitrary"),
        cost_estimate=pl.CostEstimate(flops=1_000_000, bytes_accessed=2_500_000, transcendentals=0),
        name="gate",
    )(conv, qf)


def grad_conv_kernel(own_ref, other_ref, qf_ref, gc_ref, gg_ref):
    for b in range(2):
        total = own_ref[b] + other_ref[b].astype(f32)
        gg_ref[b] = total
        gc_ref[:, :, b] = to_channels(total * qf_ref[b])


def grad_conv_call(own, other, qf):
    return pl.pallas_call(
        grad_conv_kernel,
        grid=(1024 // CB,),
        in_specs=[pos_spec, pos_spec, pos_spec],
        out_specs=[chan_spec, pos_spec],
        out_shape=[chan_shape(), pos_shape(f32)],
        compiler_params=params("arbitrary"),
        cost_estimate=pl.CostEstimate(flops=1_000_000, bytes_accessed=4_000_000, transcendentals=0),
        name="grad_conv",
    )(own, other, qf)


def unpack_kernel(gp_ref, kf_ref, vf_ref, gpp_ref, first_ref):
    for b in range(2):
        grad = to_positions(gp_ref[:, :, b])
        gpp_ref[b] = grad.astype(bf16)
        first_ref[0, b] = (grad[:HALO] * vf_ref[b]).astype(bf16)
        first_ref[1, b] = (grad[:HALO] * kf_ref[b]).astype(bf16)


def unpack(gp, kf, vf):
    rows_spec = pl.BlockSpec((2, HALO, CB), lambda c: (0, 0, c))
    return pl.pallas_call(
        unpack_kernel,
        grid=(1024 // CB,),
        in_specs=[chan_spec, rows_spec, rows_spec],
        out_specs=[pos_spec, pl.BlockSpec((2, 2, HALO, CB), lambda c: (0, 0, 0, c))],
        out_shape=[pos_shape(bf16), jax.ShapeDtypeStruct((2, 2, HALO, 1024), bf16)],
        compiler_params=params("arbitrary"),
        cost_estimate=pl.CostEstimate(flops=500_000, bytes_accessed=1_200_000, transcendentals=0),
        name="unpack",
    )(gp, kf, vf)


def backward_taps(grad, halo, taps, first):
    ext = jnp.concatenate([grad, halo.astype(f32)], axis=0)
    total = taps[first : first + 1] * grad
    for j in range(1, TAPS):
        total = total + taps[first + j : first + j + 1] * ext[j : j + BLK]
    return total.astype(bf16)


def grad_query_kernel(taps_ref, halo_ref, gg_ref, conv_ref, out_ref):
    taps = spread_taps(taps_ref[...], pl.program_id(0))
    for b in range(2):
        out_ref[b] = backward_taps(
            gg_ref[b] * conv_ref[b].astype(f32), halo_ref[0, b], taps, 0
        )


def grad_query_call(taps, halo, gg, conv):
    return pl.pallas_call(
        grad_query_kernel,
        grid=(1024 // CB,),
        in_specs=[
            taps_spec,
            pl.BlockSpec((1, 2, HALO, CB), lambda c: (0, 0, 0, c)),
            pos_spec,
            pos_spec,
        ],
        out_specs=pos_spec,
        out_shape=pos_shape(bf16),
        compiler_params=params("arbitrary"),
        cost_estimate=pl.CostEstimate(flops=4_000_000, bytes_accessed=2_100_000, transcendentals=0),
        name="grad_query",
    )(taps, halo, gg, conv)


def grad_kv_kernel(taps_ref, halo_ref, gp_ref, kf_ref, vf_ref, gk_ref, gv_ref):
    taps = spread_taps(taps_ref[...], pl.program_id(0))
    for b in range(2):
        grad = gp_ref[b].astype(f32)
        gk_ref[b] = backward_taps(grad * vf_ref[b], halo_ref[0, b], taps, TAPS)
        gv_ref[b] = backward_taps(grad * kf_ref[b], halo_ref[1, b], taps, 2 * TAPS)


def grad_kv_call(taps, halo, gp, kf, vf):
    return pl.pallas_call(
        grad_kv_kernel,
        grid=(1024 // CB,),
        in_specs=[
            taps_spec,
            pl.BlockSpec((2, 2, HALO, CB), lambda c: (0, 0, 0, c)),
            pos_spec,
            pos_spec,
            pos_spec,
        ],
        out_specs=[pos_spec, pos_spec],
        out_shape=[pos_shape(bf16), pos_shape(bf16)],
        compiler_params=params("arbitrary"),
        cost_estimate=pl.CostEstimate(flops=8_000_000, bytes_accessed=4_000_000, transcendentals=0),
        name="grad_kv",
    )(taps, halo, gp, kf, vf)


def vmem(count=1):
    return [pl.BlockSpec(memory_space=pltpu.VMEM)] * count


smem = pl.BlockSpec(memory_space=pltpu.SMEM)


def whole(kernel, name, ins, outs, flops=0, scratch=(), index=True):
    size = sum(a.size * a.dtype.itemsize for a in ins)
    size += sum(a.size * jnp.dtype(a.dtype).itemsize for a in outs)
    return pl.pallas_call(
        kernel,
        in_specs=([smem] if index else []) + vmem(len(ins) - int(index)),
        out_specs=vmem(len(outs)),
        out_shape=list(outs),
        scratch_shapes=list(scratch),
        compiler_params=pltpu.CompilerParams(vmem_limit_bytes=48 * 1024 * 1024),
        cost_estimate=pl.CostEstimate(flops=flops, bytes_accessed=size, transcendentals=0),
        name=name,
    )(*ins)


def shape(dims, kind=bf16):
    return jax.ShapeDtypeStruct(dims, kind)


def prep_kernel(at, q_ref, k_ref, v_ref, w_ref, g_ref, last_ref, wa_ref, wb_ref, mine_ref, theirs_ref):
    first_core = at[3] == 0
    for i, src in enumerate((q_ref, k_ref, v_ref)):
        last_ref[i] = src[...]
    wa_ref[...] = w_ref[:, :512]
    wb_ref[...] = w_ref[:, 512:]
    for x in range(NX):
        lo = g_ref[:, 256 * x : 256 * x + BLK]
        hi = g_ref[:, 256 * x + BLK : 256 * x + 256]
        mine_ref[:, BLK * x : BLK * x + BLK] = jnp.where(first_core, lo, hi)
        theirs_ref[:, BLK * x : BLK * x + BLK] = jnp.where(first_core, hi, lo)


def prep(at, q, k, v, weight, grad_out):
    rows = pl.BlockSpec((2, HALO, 1024), lambda i: (0, BLK // HALO - 1, 0))
    full = lambda dims: pl.BlockSpec(dims, lambda i: (0,) * len(dims))
    return pl.pallas_call(
        prep_kernel,
        grid=(1,),
        in_specs=[smem, rows, rows, rows, full((BLK, 1024)), full((256, 1024))],
        out_specs=[full((3, 2, HALO, 1024)), full((BLK, 512)), full((BLK, 512)), full((256, 512)), full((256, 512))],
        out_shape=[
            shape((3, 2, HALO, 1024)),
            shape((BLK, 512)),
            shape((BLK, 512)),
            shape((256, 512)),
            shape((256, 512)),
        ],
        compiler_params=params("arbitrary"),
        name="prep",
    )(at, q, k, v, weight, grad_out)


def grad_gated_kernel(at, *refs):
    cols, part_a, part_b = refs[:4], refs[4:8], refs[8:12]
    own_ref, other_ref, cols_ref, w_ref = refs[12:]
    for d in range(4):
        cols_ref[(at[2] + 4 - d) & 3] = cols[d][...]
        for e in range(4):
            w_ref[(at[0] + 4 - d) & 3, (at[1] + 4 - e) & 3, :, :512] = part_a[d][e]
            w_ref[(at[0] + 4 - e) & 3, (at[1] + 4 - d) & 3, :, 512:] = part_b[d][e]

    def step(n, carry):
        lanes = pl.ds(pl.multiple_of(n * 256, 256), 256)
        total = jnp.zeros((512, 256), f32)
        for y in range(NY):
            total = total + jnp.dot(
                cols_ref[y], w_ref[y, :, :, lanes].reshape(512, 256), preferred_element_type=f32
            )
        own_ref[:, lanes] = total[:256]
        other_ref[:, lanes] = total[256:].astype(bf16)
        return carry

    lax.fori_loop(0, 4, step, 0)


def mixed_kernel(at, own_g, other_g, w_ref, *outs):
    for d in range(4):
        block = w_ref[(at[2] + d) & 3].reshape(512, 1024)
        for i, src in enumerate((own_g, other_g)):
            part = lax.dot_general(
                src[...], block, (((1,), (1,)), ((), ())), preferred_element_type=f32
            )
            outs[d][256 * i : 256 * i + 256] = part.astype(outs[d].dtype)


def mixed_sum_kernel(own, a_ref, b_ref, c_ref, keep_ref, send_ref):
    total = own[...] + a_ref[...].astype(f32) + b_ref[...].astype(f32) + c_ref[...].astype(f32)
    keep_ref[...] = total[:256].astype(bf16)
    send_ref[...] = total[256:].astype(bf16)


def mixed_out_kernel(at, keep_ref, came_ref, out_ref):
    first_core = at[3] == 0
    for x in range(NX):
        keep = keep_ref[:, BLK * x : BLK * x + BLK]
        came = came_ref[:, BLK * x : BLK * x + BLK]
        out_ref[:, 256 * x : 256 * x + BLK] = jnp.where(first_core, keep, came)
        out_ref[:, 256 * x + BLK : 256 * x + 256] = jnp.where(first_core, came, keep)


def weight_grad_kernel(at, cols_ref, own_g, other_g, *refs):
    outs_a, outs_b, held_b = refs[:4], refs[4:8], refs[8]
    for d in range(4):
        cols = cols_ref[(at[0] + d) & 3]
        for n in range(2):
            lanes = slice(512 * n, 512 * n + 512)
            total = lax.dot_general(
                cols[:256], own_g[:, lanes], (((0,), (0,)), ((), ())), preferred_element_type=f32
            ) + lax.dot_general(
                cols[256:], other_g[:, lanes], (((0,), (0,)), ((), ())), preferred_element_type=f32
            )
            total = total.astype(bf16)
            for x in range(NX):
                block = total[BLK * x : BLK * x + BLK]
                if n == 0:
                    outs_a[d][(x + 4 - at[1]) & 3] = block
                else:
                    held_b[(x + 4 - at[1]) & 3, d] = block
    for e in range(4):
        outs_b[e][...] = held_b[e]


def sum_split_kernel(*refs):
    parts, outs = refs[:4], refs[4:]
    for e in range(4):
        total = parts[0][e].astype(f32)
        for part in parts[1:]:
            total = total + part[e].astype(f32)
        outs[e][...] = total.astype(outs[e].dtype)


def weight_out_kernel(*refs):
    out_ref = refs[8]
    for n in range(2):
        total = refs[4 * n][...]
        for part in refs[4 * n + 1 : 4 * n + 4]:
            total = total + part[...].astype(f32)
        out_ref[:, 512 * n : 512 * n + 512] = total


def exchange(value):
    return lax.all_to_all(value, "context", split_axis=0, concat_axis=0, tiled=True)


def body(query_in, key_in, value_in, short_filter, long_filter, out_weight, grad_out):
    batches, rows, channels = query_in.shape
    scale = float(batches * rows * NCTX * GROUP) ** (-0.5)
    ctx = lax.axis_index("context")
    at_y = lax.axis_index("tensor")
    at = jnp.stack([ctx // (NC * NX), (ctx // NC) % NX, at_y, ctx % NC]).astype(jnp.int32)
    positions = batches * rows
    half = channels // 2

    taps = jnp.pad(short_filter.reshape(3 * TAPS, channels // GROUP), ((0, 3), (0, 0)))
    last, w_a, w_b, mine, theirs = prep(
        at, query_in, key_in, value_in, out_weight, grad_out.reshape(positions, channels)
    )
    before = next_context(last, 1)

    w_a = jnp.stack(around(w_a, move_x))
    w_b = jnp.stack(around(w_b, move_z))
    w_a = around(w_a, move_z)
    w_b = around(w_b, move_x)

    columns = around(jnp.concatenate([mine, swap_core(theirs)]), move_y)

    tiles = toeplitz_tiles(long_filter)
    prod, qf, kf, vf = featurize(taps, before, query_in, key_in, value_in)
    prod = exchange(prod)
    conv = exchange(convolve(conv_kernel, "conv", prod, tiles))
    gated, conv = gate(conv, qf)
    gated_own = gated.reshape(positions, channels)
    gated_other = swap_core(gated_own)

    own, other, columns, weights = whole(
        grad_gated_kernel,
        "grad_gated",
        [at, *columns, *w_a, *w_b],
        [
            shape((positions, channels), f32),
            shape((positions, channels)),
            shape((NY, 2 * positions, half)),
            shape((NZ, NX, BLK, channels)),
        ],
        flops=2_200_000_000,
    )
    other = swap_core(other)
    grad_conv, grad_gated = grad_conv_call(
        own.reshape(query_in.shape), other.reshape(query_in.shape), qf
    )
    grad_conv = exchange(grad_conv)

    part = shape((4, BLK, half))
    sums = whole(
        weight_grad_kernel,
        "grad_weight",
        [at, columns, gated_own, gated_other],
        [part] * 8,
        flops=2_200_000_000,
        scratch=[pltpu.VMEM((4, 4, BLK, half), bf16)],
    )
    sums_a = deliver(sums[:4], move_z)
    sums_b = deliver(sums[4:], move_x)

    mixed = whole(
        mixed_kernel,
        "mixed",
        [at, gated_own, gated_other, weights],
        [shape((2 * positions, half), f32)] + [shape((2 * positions, half))] * 3,
        flops=2_200_000_000,
    )
    mixed = deliver(mixed, move_y)
    pieces = [shape((BLK, half), f32)] + [shape((BLK, half))] * 3
    sums_a = deliver(whole(sum_split_kernel, "sum_a", sums_a, pieces, index=False), move_x)
    sums_b = deliver(whole(sum_split_kernel, "sum_b", sums_b, pieces, index=False), move_z)
    keep, send = whole(
        mixed_sum_kernel, "mixed_sum", mixed, [shape((positions, half))] * 2, index=False
    )
    (mixed_out,) = whole(
        mixed_out_kernel, "mixed_out", [at, keep, swap_core(send)], [shape((positions, channels))]
    )
    mixed_out = mixed_out.reshape(query_in.shape)
    (grad_weight,) = whole(
        weight_out_kernel,
        "weight_out",
        [*sums_a, *sums_b],
        [shape((BLK, channels), f32)],
        index=False,
    )

    first_q = (grad_gated[:, :HALO] * conv[:, :HALO].astype(f32)).astype(bf16)[None]
    after_q = next_context(first_q, -1)
    grad_query = grad_query_call(taps, after_q, grad_gated, conv)

    grad_product = exchange(convolve(corr_kernel, "corr", grad_conv, tiles))
    grad_long = grad_long_call(scale, prod, grad_conv)
    grad_product, first_kv = unpack(grad_product, kf, vf)
    after_kv = next_context(first_kv, -1)
    grad_key, grad_value = grad_kv_call(taps, after_kv, grad_product, kf, vf)
    return (mixed_out, grad_query, grad_key, grad_value, grad_weight, grad_long)


def solution(mesh):
    act = P(None, "context", "tensor")
    in_specs = (
        act,
        act,
        act,
        P(None, None, "tensor"),
        P(("tensor", "context"), None),
        P("context", "tensor"),
        act,
    )
    out_specs = (act, act, act, act, P("context", "tensor"), P(("tensor", "context"), None))
    return jax.shard_map(body, mesh=mesh, in_specs=in_specs, out_specs=out_specs, check_vma=False)
```

```python
import functools

import jax
import jax.numpy as jnp
from jax import lax
from jax.experimental import pallas as pl
from jax.experimental.pallas import tpu as pltpu
from jax.sharding import PartitionSpec as P

GROUP = 16
TAPS = 7
HALO = 16
NZ, NX, NC, NY = 4, 4, 2, 4
NCTX = NZ * NX * NC
BLK = 128
CB = 256
VMEM_BYTES = 48 * 1024 * 1024
f32 = jnp.float32
bf16 = jnp.bfloat16


def move_ctx(value, dz, dx, dc):
    pairs = []
    for z in range(NZ):
        for x in range(NX):
            for c in range(NC):
                src = (z * NX + x) * NC + c
                dst = (((z + dz) % NZ) * NX + (x + dx) % NX) * NC + (c + dc) % NC
                pairs.append((src, dst))
    return lax.ppermute(value, "context", pairs)


def move_z(value, d):
    return move_ctx(value, d, 0, 0)


def move_x(value, d):
    return move_ctx(value, 0, d, 0)


def swap_core(value):
    return move_ctx(value, 0, 0, 1)


def move_y(value, d):
    return lax.ppermute(value, "tensor", [(i, (i + d) % NY) for i in range(NY)])


def next_context(value, steps):
    first, last = (max(0, -steps), min(NCTX, NCTX - steps))
    return lax.ppermute(value, "context", [(s, s + steps) for s in range(first, last)])


def around(value, move, count=4):
    return [value] + [move(value, d) for d in range(1, count)]


def deliver(parts, move):
    return [parts[0]] + [move(part, d) for d, part in enumerate(parts) if d > 0]


def params(*sem):
    return pltpu.CompilerParams(dimension_semantics=sem, vmem_limit_bytes=VMEM_BYTES)


def toeplitz_kernel(filter_ref, tile_ref):
    taps = jnp.concatenate([jnp.zeros((1, BLK), f32), filter_ref[0]], axis=1)
    blocks = taps.shape[1] // BLK - 1
    tile_ref[0, 0, BLK:, :BLK] = jnp.zeros((BLK, BLK), bf16)
    for e in range(blocks):
        window = jnp.broadcast_to(taps[:, BLK * e : BLK * (e + 2)], (BLK, 2 * BLK))
        rolled = pltpu.roll(window, 0, 1, stride=1, stride_axis=0)
        piece = rolled[:, BLK:].astype(bf16)
        if e % 2 == 0:
            tile_ref[0, e // 2, :BLK, :BLK] = piece
            tile_ref[0, e // 2, BLK:, BLK:] = piece
        else:
            tile_ref[0, e // 2, :BLK, BLK:] = piece
            if e + 1 < blocks:
                tile_ref[0, e // 2 + 1, BLK:, :BLK] = piece


def toeplitz_tiles(long_filter):
    groups, length = long_filter.shape
    tiles = length // (2 * BLK)
    return pl.pallas_call(
        toeplitz_kernel,
        grid=(groups,),
        in_specs=[pl.BlockSpec((1, 1, length), lambda g: (g, 0, 0))],
        out_specs=pl.BlockSpec((1, tiles, 2 * BLK, 2 * BLK), lambda g: (g, 0, 0, 0)),
        out_shape=jax.ShapeDtypeStruct((groups, tiles, 2 * BLK, 2 * BLK), bf16),
        compiler_params=params("arbitrary"),
        cost_estimate=pl.CostEstimate(flops=8_000_000, bytes_accessed=4_300_000, transcendentals=0),
        name="toeplitz_tiles",
    )(long_filter[:, None, :])


def spread_taps(taps, block):
    rows = lax.broadcasted_iota(jnp.int32, (taps.shape[1], CB), 0)
    cols = lax.broadcasted_iota(jnp.int32, (taps.shape[1], CB), 1)
    spread = (rows == ((block * CB + cols) >> 4)).astype(f32)
    return jnp.dot(taps, spread, precision=lax.Precision.HIGHEST, preferred_element_type=f32)


def to_channels(value):
    return value.T.reshape(CB // (2 * GROUP), 2, GROUP, BLK).astype(bf16)


def to_positions(value):
    return value.astype(f32).reshape(CB, BLK).T


def featurize_kernel(taps_ref, halo_ref, q_ref, k_ref, v_ref, prod_ref, qf_ref, kf_ref, vf_ref):
    taps = spread_taps(taps_ref[...], pl.program_id(0))
    for b in range(2):
        feats = []
        for i, (src, dst) in enumerate(((q_ref, qf_ref), (k_ref, kf_ref), (v_ref, vf_ref))):
            ext = jnp.concatenate([halo_ref[i, b].astype(f32), src[b].astype(f32)], axis=0)
            total = taps[7 * i : 7 * i + 1] * ext[HALO:]
            for j in range(1, TAPS):
                total = total + taps[7 * i + j : 7 * i + j + 1] * ext[HALO - j : HALO - j + BLK]
            dst[b] = total
            feats.append(total)
        prod_ref[:, :, b] = to_channels(feats[1] * feats[2])


chan_spec = pl.BlockSpec((CB // (2 * GROUP), 2, 2, GROUP, BLK), lambda c: (c, 0, 0, 0, 0))
pos_spec = pl.BlockSpec((2, BLK, CB), lambda c: (0, 0, c))
taps_spec = pl.BlockSpec((24, 64), lambda c: (0, 0))
halo_spec = pl.BlockSpec((3, 2, HALO, CB), lambda c: (0, 0, 0, c))


def chan_shape():
    return jax.ShapeDtypeStruct((NCTX, 2, 2, GROUP, BLK), bf16)


def pos_shape(kind):
    return jax.ShapeDtypeStruct((2, BLK, 1024), kind)


def featurize(taps, halo, q, k, v):
    return pl.pallas_call(
        featurize_kernel,
        grid=(1024 // CB,),
        in_specs=[taps_spec, halo_spec, pos_spec, pos_spec, pos_spec],
        out_specs=[chan_spec, pos_spec, pos_spec, pos_spec],
        out_shape=[chan_shape(), pos_shape(f32), pos_shape(f32), pos_shape(f32)],
        compiler_params=pltpu.CompilerParams(vmem_limit_bytes=62 * 1024 * 1024),
        cost_estimate=pl.CostEstimate(flops=12_000_000, bytes_accessed=5_500_000, transcendentals=0),
        name="featurize",
    )(taps, halo, q, k, v)


def fold(src_ref, dst_ref):
    for i in range(NCTX // 2):
        dst_ref[32 * i : 32 * i + 32, :BLK] = src_ref[2 * i, 0].reshape(32, BLK)
        dst_ref[32 * i : 32 * i + 32, BLK:] = src_ref[2 * i + 1, 0].reshape(32, BLK)


def unfold(acc_ref, dst_ref):
    for i in range(NCTX // 2):
        rows = acc_ref[32 * i : 32 * i + 32].astype(bf16)
        dst_ref[2 * i, 0] = rows[:, :BLK].reshape(2, GROUP, BLK)
        dst_ref[2 * i + 1, 0] = rows[:, BLK:].reshape(2, GROUP, BLK)


def conv_kernel(x_ref, tile_ref, out_ref, x_s, acc_s):
    fold(x_ref, x_s)
    rows = x_s.shape[0]
    for d in range(rows // 32):
        term = jnp.dot(x_s[: rows - 32 * d], tile_ref[0, d], preferred_element_type=f32)
        if d == 0:
            acc_s[...] = term
        else:
            acc_s[32 * d :] += term
    unfold(acc_s, out_ref)


def corr_kernel(x_ref, tile_ref, out_ref, x_s, acc_s):
    fold(x_ref, x_s)
    rows = x_s.shape[0]
    for d in range(rows // 32):
        term = lax.dot_general(
            x_s[32 * d :], tile_ref[0, d], (((1,), (1,)), ((), ())), preferred_element_type=f32
        )
        if d == 0:
            acc_s[...] = term
        else:
            acc_s[: rows - 32 * d] += term
    unfold(acc_s, out_ref)


group_spec = pl.BlockSpec((NCTX, 1, 2, GROUP, BLK), lambda g: (0, g, 0, 0, 0))
tile_spec = pl.BlockSpec((1, 16, 2 * BLK, 2 * BLK), lambda g: (g, 0, 0, 0))


def convolve(kernel, name, x, tiles):
    return pl.pallas_call(
        kernel,
        grid=(2,),
        in_specs=[group_spec, tile_spec],
        out_specs=group_spec,
        out_shape=chan_shape(),
        scratch_shapes=[pltpu.VMEM((512, 256), bf16), pltpu.VMEM((512, 256), f32)],
        compiler_params=params("arbitrary"),
        cost_estimate=pl.CostEstimate(flops=1_100_000_000, bytes_accessed=5_300_000, transcendentals=0),
        name=name,
    )(x, tiles)


def grad_long_kernel(scale, p_ref, g_ref, out_ref, p_s, g_s):
    fold(p_ref, p_s)
    fold(g_ref, g_s)
    g_s[512:] = jnp.zeros((512, 256), bf16)
    rows = lax.broadcasted_iota(jnp.int32, (256, 256), 0)
    cols = lax.broadcasted_iota(jnp.int32, (256, 256), 1)
    flip = (rows + cols == 255).astype(bf16)
    back = lax.dot_general(
        flip, p_s[...], (((1,), (1,)), ((), ())), preferred_element_type=f32
    ).astype(bf16)

    def diagonals(block):
        padded = jnp.concatenate([block, jnp.zeros((BLK, BLK), f32)], axis=1)
        rolled = pltpu.roll(padded, 1, 1, stride=1, stride_axis=0)
        return jnp.sum(rolled, axis=0, keepdims=True)

    def gram(d):
        return jnp.dot(back, g_s[32 * d : 32 * d + 512], preferred_element_type=f32)

    here = gram(0)
    lag = diagonals(here[BLK:, :BLK] + here[:BLK, BLK:])
    for d in range(16):
        later = gram(d + 1) if d < 15 else None
        cross = here[BLK:, BLK:]
        if later is not None:
            cross = cross + later[:BLK, :BLK]
        odd = diagonals(cross)
        out_ref[0, :, 256 * d : 256 * d + BLK] = scale * (lag[:, BLK:] + odd[:, :BLK])
        if later is not None:
            lag = diagonals(later[BLK:, :BLK] + later[:BLK, BLK:])
            out_ref[0, :, 256 * d + BLK : 256 * d + 256] = scale * (odd[:, BLK:] + lag[:, :BLK])
        else:
            out_ref[0, :, 256 * d + BLK : 256 * d + 256] = scale * odd[:, BLK:]
        here = later


def grad_long_call(scale, prod, grad_conv):
    return pl.pallas_call(
        functools.partial(grad_long_kernel, scale),
        grid=(2,),
        in_specs=[group_spec, group_spec],
        out_specs=pl.BlockSpec((1, 1, NCTX * BLK), lambda g: (g, 0, 0)),
        out_shape=jax.ShapeDtypeStruct((2, 1, NCTX * BLK), f32),
        scratch_shapes=[pltpu.VMEM((512, 256), bf16), pltpu.VMEM((1024, 256), bf16)],
        compiler_params=params("arbitrary"),
        cost_estimate=pl.CostEstimate(flops=2_200_000_000, bytes_accessed=1_200_000, transcendentals=0),
        name="grad_long",
    )(prod, grad_conv)[:, 0]


def gate_kernel(conv_ref, qf_ref, gated_ref, convp_ref):
    for b in range(2):
        conv = to_positions(conv_ref[:, :, b])
        convp_ref[b] = conv.astype(bf16)
        gated_ref[b] = (qf_ref[b] * conv).astype(bf16)


def gate(conv, qf):
    return pl.pallas_call(
        gate_kernel,
        grid=(1024 // CB,),
        in_specs=[chan_spec, pos_spec],
        out_specs=[pos_spec, pos_spec],
        out_shape=[pos_shape(bf16), pos_shape(bf16)],
        compiler_params=params("arbitrary"),
        cost_estimate=pl.CostEstimate(flops=1_000_000, bytes_accessed=2_500_000, transcendentals=0),
        name="gate",
    )(conv, qf)


def grad_conv_kernel(own_ref, other_ref, qf_ref, gc_ref, gg_ref):
    for b in range(2):
        total = own_ref[b] + other_ref[b].astype(f32)
        gg_ref[b] = total
        gc_ref[:, :, b] = to_channels(total * qf_ref[b])


def grad_conv_call(own, other, qf):
    return pl.pallas_call(
        grad_conv_kernel,
        grid=(1024 // CB,),
        in_specs=[pos_spec, pos_spec, pos_spec],
        out_specs=[chan_spec, pos_spec],
        out_shape=[chan_shape(), pos_shape(f32)],
        compiler_params=params("arbitrary"),
        cost_estimate=pl.CostEstimate(flops=1_000_000, bytes_accessed=4_000_000, transcendentals=0),
        name="grad_conv",
    )(own, other, qf)


def unpack_kernel(gp_ref, kf_ref, vf_ref, gpp_ref, first_ref):
    for b in range(2):
        grad = to_positions(gp_ref[:, :, b])
        gpp_ref[b] = grad.astype(bf16)
        first_ref[0, b] = (grad[:HALO] * vf_ref[b]).astype(bf16)
        first_ref[1, b] = (grad[:HALO] * kf_ref[b]).astype(bf16)


def unpack(gp, kf, vf):
    rows_spec = pl.BlockSpec((2, HALO, CB), lambda c: (0, 0, c))
    return pl.pallas_call(
        unpack_kernel,
        grid=(1024 // CB,),
        in_specs=[chan_spec, rows_spec, rows_spec],
        out_specs=[pos_spec, pl.BlockSpec((2, 2, HALO, CB), lambda c: (0, 0, 0, c))],
        out_shape=[pos_shape(bf16), jax.ShapeDtypeStruct((2, 2, HALO, 1024), bf16)],
        compiler_params=params("arbitrary"),
        cost_estimate=pl.CostEstimate(flops=500_000, bytes_accessed=1_200_000, transcendentals=0),
        name="unpack",
    )(gp, kf, vf)


def backward_taps(grad, halo, taps, first):
    ext = jnp.concatenate([grad, halo.astype(f32)], axis=0)
    total = taps[first : first + 1] * grad
    for j in range(1, TAPS):
        total = total + taps[first + j : first + j + 1] * ext[j : j + BLK]
    return total.astype(bf16)


def grad_query_kernel(taps_ref, halo_ref, gg_ref, conv_ref, out_ref):
    taps = spread_taps(taps_ref[...], pl.program_id(0))
    for b in range(2):
        out_ref[b] = backward_taps(
            gg_ref[b] * conv_ref[b].astype(f32), halo_ref[0, b], taps, 0
        )


def grad_query_call(taps, halo, gg, conv):
    return pl.pallas_call(
        grad_query_kernel,
        grid=(1024 // CB,),
        in_specs=[
            taps_spec,
            pl.BlockSpec((1, 2, HALO, CB), lambda c: (0, 0, 0, c)),
            pos_spec,
            pos_spec,
        ],
        out_specs=pos_spec,
        out_shape=pos_shape(bf16),
        compiler_params=params("arbitrary"),
        cost_estimate=pl.CostEstimate(flops=4_000_000, bytes_accessed=2_100_000, transcendentals=0),
        name="grad_query",
    )(taps, halo, gg, conv)


def grad_kv_kernel(taps_ref, halo_ref, gp_ref, kf_ref, vf_ref, gk_ref, gv_ref):
    taps = spread_taps(taps_ref[...], pl.program_id(0))
    for b in range(2):
        grad = gp_ref[b].astype(f32)
        gk_ref[b] = backward_taps(grad * vf_ref[b], halo_ref[0, b], taps, TAPS)
        gv_ref[b] = backward_taps(grad * kf_ref[b], halo_ref[1, b], taps, 2 * TAPS)


def grad_kv_call(taps, halo, gp, kf, vf):
    return pl.pallas_call(
        grad_kv_kernel,
        grid=(1024 // CB,),
        in_specs=[
            taps_spec,
            pl.BlockSpec((2, 2, HALO, CB), lambda c: (0, 0, 0, c)),
            pos_spec,
            pos_spec,
            pos_spec,
        ],
        out_specs=[pos_spec, pos_spec],
        out_shape=[pos_shape(bf16), pos_shape(bf16)],
        compiler_params=params("arbitrary"),
        cost_estimate=pl.CostEstimate(flops=8_000_000, bytes_accessed=4_000_000, transcendentals=0),
        name="grad_kv",
    )(taps, halo, gp, kf, vf)


def vmem(count=1):
    return [pl.BlockSpec(memory_space=pltpu.VMEM)] * count


smem = pl.BlockSpec(memory_space=pltpu.SMEM)


def whole(kernel, name, ins, outs, flops=0, scratch=(), index=True):
    size = sum(a.size * a.dtype.itemsize for a in ins)
    size += sum(a.size * jnp.dtype(a.dtype).itemsize for a in outs)
    return pl.pallas_call(
        kernel,
        in_specs=([smem] if index else []) + vmem(len(ins) - int(index)),
        out_specs=vmem(len(outs)),
        out_shape=list(outs),
        scratch_shapes=list(scratch),
        compiler_params=pltpu.CompilerParams(vmem_limit_bytes=VMEM_BYTES),
        cost_estimate=pl.CostEstimate(flops=flops, bytes_accessed=size, transcendentals=0),
        name=name,
    )(*ins)


def shape(dims, kind=bf16):
    return jax.ShapeDtypeStruct(dims, kind)


def prep_kernel(at, q_ref, k_ref, v_ref, g_ref, last_ref, mine_ref, theirs_ref):
    first_core = at[3] == 0
    for i, src in enumerate((q_ref, k_ref, v_ref)):
        last_ref[i] = src[...]
    for x in range(NX):
        lo = g_ref[:, 256 * x : 256 * x + BLK]
        hi = g_ref[:, 256 * x + BLK : 256 * x + 256]
        mine_ref[:, BLK * x : BLK * x + BLK] = jnp.where(first_core, lo, hi)
        theirs_ref[:, BLK * x : BLK * x + BLK] = jnp.where(first_core, hi, lo)


def prep(at, q, k, v, grad_out):
    rows = pl.BlockSpec((2, HALO, 1024), lambda i: (0, BLK // HALO - 1, 0))
    full = lambda dims: pl.BlockSpec(dims, lambda i: (0,) * len(dims))
    return pl.pallas_call(
        prep_kernel,
        grid=(1,),
        in_specs=[smem, rows, rows, rows, full((256, 1024))],
        out_specs=[full((3, 2, HALO, 1024)), full((256, 512)), full((256, 512))],
        out_shape=[
            shape((3, 2, HALO, 1024)),
            shape((256, 512)),
            shape((256, 512)),
        ],
        compiler_params=pltpu.CompilerParams(vmem_limit_bytes=62 * 1024 * 1024),
        name="prep",
    )(at, q, k, v, grad_out)


def grad_gated_kernel(at, c0, c1, c2, c3, w_ref, own_ref, other_ref):
    total = jnp.zeros((512, 256), f32)
    for d, cols in enumerate((c0, c1, c2, c3)):
        total = total + jnp.dot(
            cols[...], w_ref[(at[2] + 4 - d) & 3], preferred_element_type=f32
        )
    own_ref[...] = total[:256]
    other_ref[...] = total[256:].astype(bf16)


def grad_gated_call(at, columns, weights):
    fixed = pl.BlockSpec((512, 512), lambda n: (0, 0))
    return pl.pallas_call(
        grad_gated_kernel,
        grid=(4,),
        in_specs=[smem] + [fixed] * 4 + [pl.BlockSpec((4, 512, 256), lambda n: (0, 0, n))],
        out_specs=[pl.BlockSpec((256, 256), lambda n: (0, n))] * 2,
        out_shape=[shape((256, 1024), f32), shape((256, 1024))],
        compiler_params=params("arbitrary"),
        cost_estimate=pl.CostEstimate(flops=2_200_000_000, bytes_accessed=7_800_000, transcendentals=0),
        name="grad_gated",
    )(at, *columns, weights)


def mixed_kernel(at, own_g, other_g, w_ref, *outs):
    for d in range(4):
        block = w_ref[(at[2] + d) & 3]
        for i, src in enumerate((own_g, other_g)):
            part = lax.dot_general(
                src[...], block, (((1,), (1,)), ((), ())), preferred_element_type=f32
            )
            outs[d][256 * i : 256 * i + 256] = part.astype(outs[d].dtype)


def mixed_call(at, own, other, weights):
    fixed = pl.BlockSpec((256, 1024), lambda n: (0, 0))
    return pl.pallas_call(
        mixed_kernel,
        grid=(2,),
        in_specs=[smem, fixed, fixed, pl.BlockSpec((4, 256, 1024), lambda n: (0, n, 0))],
        out_specs=[pl.BlockSpec((512, 256), lambda n: (0, n))] * 4,
        out_shape=[shape((512, 512), f32)] + [shape((512, 512))] * 3,
        compiler_params=params("arbitrary"),
        cost_estimate=pl.CostEstimate(flops=2_200_000_000, bytes_accessed=7_800_000, transcendentals=0),
        name="mixed",
    )(at, own, other, weights)


def mixed_sum_kernel(own, a_ref, b_ref, c_ref, keep_ref, send_ref):
    total = own[...] + a_ref[...].astype(f32) + b_ref[...].astype(f32) + c_ref[...].astype(f32)
    keep_ref[...] = total[:256].astype(bf16)
    send_ref[...] = total[256:].astype(bf16)


def mixed_out_kernel(at, keep_ref, came_ref, out_ref):
    first_core = at[3] == 0
    for x in range(NX):
        keep = keep_ref[:, BLK * x : BLK * x + BLK]
        came = came_ref[:, BLK * x : BLK * x + BLK]
        out_ref[:, 256 * x : 256 * x + BLK] = jnp.where(first_core, keep, came)
        out_ref[:, 256 * x + BLK : 256 * x + 256] = jnp.where(first_core, came, keep)


def weight_grad_kernel(at, c0, c1, c2, c3, own_g, other_g, out_ref):
    for d, cols in enumerate((c0, c1, c2, c3)):
        total = 0.0
        for i, src in enumerate((own_g, other_g)):
            total = total + lax.dot_general(
                cols[256 * i : 256 * i + 256],
                src[...],
                (((0,), (0,)), ((), ())),
                preferred_element_type=f32,
            )
        out_ref[(at[2] + 4 - d) & 3] = total.astype(bf16)


def weight_grad_call(at, columns, own, other):
    fixed = pl.BlockSpec((512, 512), lambda n: (0, 0))
    return pl.pallas_call(
        weight_grad_kernel,
        grid=(2,),
        in_specs=[smem] + [fixed] * 4 + [pl.BlockSpec((256, 512), lambda n: (0, n))] * 2,
        out_specs=pl.BlockSpec((4, 512, 512), lambda n: (0, 0, n)),
        out_shape=shape((4, 512, 1024)),
        compiler_params=params("arbitrary"),
        cost_estimate=pl.CostEstimate(flops=2_200_000_000, bytes_accessed=7_800_000, transcendentals=0),
        name="grad_weight",
    )(at, *columns, own, other)


def exchange(value):
    return lax.all_to_all(value, "context", split_axis=0, concat_axis=0, tiled=True)


def body(query_in, key_in, value_in, short_filter, long_filter, out_weight, grad_out):
    batches, rows, channels = query_in.shape
    scale = float(batches * rows * NCTX * GROUP) ** (-0.5)
    ctx = lax.axis_index("context")
    at_y = lax.axis_index("tensor")
    at = jnp.stack([ctx // (NC * NX), (ctx // NC) % NX, at_y, ctx % NC]).astype(jnp.int32)
    positions = batches * rows
    half = channels // 2

    taps = jnp.pad(short_filter.reshape(3 * TAPS, channels // GROUP), ((0, 3), (0, 0)))
    same_core = [list(range(c, NCTX, NC)) for c in range(NC)]
    weights = lax.all_gather(
        out_weight,
        "context",
        axis=0,
        tiled=True,
        axis_index_groups=same_core,
    ).reshape(NY, half, channels)
    last, mine, theirs = prep(
        at, query_in, key_in, value_in, grad_out.reshape(positions, channels)
    )
    before = next_context(last, 1)

    columns = around(jnp.concatenate([mine, swap_core(theirs)]), move_y)

    tiles = toeplitz_tiles(long_filter)
    prod, qf, kf, vf = featurize(taps, before, query_in, key_in, value_in)
    prod = exchange(prod)
    conv = exchange(convolve(conv_kernel, "conv", prod, tiles))
    gated, conv = gate(conv, qf)
    gated_own = gated.reshape(positions, channels)
    gated_other = swap_core(gated_own)

    own, other = grad_gated_call(at, columns, weights)
    other = swap_core(other)
    grad_conv, grad_gated = grad_conv_call(
        own.reshape(query_in.shape), other.reshape(query_in.shape), qf
    )
    grad_conv, gated_own = lax.optimization_barrier((grad_conv, gated_own))
    grad_conv_all = exchange(grad_conv)

    sums = weight_grad_call(at, columns, gated_own, gated_other).reshape(-1, channels)
    grad_weight = lax.psum_scatter(
        sums, "context", scatter_dimension=0, axis_index_groups=same_core, tiled=True
    ).astype(f32)

    mixed = mixed_call(at, gated_own, gated_other, weights)
    mixed = deliver(mixed, move_y)
    keep, send = whole(
        mixed_sum_kernel, "mixed_sum", mixed, [shape((positions, half))] * 2, index=False
    )
    (mixed_out,) = whole(
        mixed_out_kernel, "mixed_out", [at, keep, swap_core(send)], [shape((positions, channels))]
    )
    mixed_out = mixed_out.reshape(query_in.shape)
    first_q = (grad_gated[:, :HALO] * conv[:, :HALO].astype(f32)).astype(bf16)[None]
    after_q = next_context(first_q, -1)
    grad_query = grad_query_call(taps, after_q, grad_gated, conv)

    grad_product = exchange(convolve(corr_kernel, "corr", grad_conv_all, tiles))
    grad_long = grad_long_call(scale, prod, grad_conv_all)
    grad_product, grad_long, grad_query = lax.optimization_barrier(
        (grad_product, grad_long, grad_query)
    )
    grad_product, first_kv = unpack(grad_product, kf, vf)
    after_kv = next_context(first_kv, -1)
    grad_key, grad_value = grad_kv_call(taps, after_kv, grad_product, kf, vf)
    return (mixed_out, grad_query, grad_key, grad_value, grad_weight, grad_long)


def solution(mesh):
    act = P(None, "context", "tensor")
    in_specs = (
        act,
        act,
        act,
        P(None, None, "tensor"),
        P(("tensor", "context"), None),
        P("context", "tensor"),
        act,
    )
    out_specs = (act, act, act, act, P("context", "tensor"), P(("tensor", "context"), None))
    return jax.shard_map(body, mesh=mesh, in_specs=in_specs, out_specs=out_specs, check_vma=False)
```

```python
import functools

import jax
import jax.numpy as jnp
from jax import lax
from jax.experimental import pallas as pl
from jax.experimental.pallas import tpu as pltpu
from jax.sharding import PartitionSpec as P

GROUP = 16
TAPS = 7
HALO = 16
NZ, NX, NC, NY = 4, 4, 2, 4
NCTX = NZ * NX * NC
BLK = 128
CB = 256
VMEM_BYTES = 32 * 1024 * 1024
f32 = jnp.float32
bf16 = jnp.bfloat16


def move_ctx(value, dz, dx, dc):
    pairs = []
    for z in range(NZ):
        for x in range(NX):
            for c in range(NC):
                src = (z * NX + x) * NC + c
                dst = (((z + dz) % NZ) * NX + (x + dx) % NX) * NC + (c + dc) % NC
                pairs.append((src, dst))
    return lax.ppermute(value, "context", pairs)


def move_z(value, d):
    return move_ctx(value, d, 0, 0)


def move_x(value, d):
    return move_ctx(value, 0, d, 0)


def swap_core(value):
    return move_ctx(value, 0, 0, 1)


def move_y(value, d):
    return lax.ppermute(value, "tensor", [(i, (i + d) % NY) for i in range(NY)])


def next_context(value, steps):
    first, last = (max(0, -steps), min(NCTX, NCTX - steps))
    return lax.ppermute(value, "context", [(s, s + steps) for s in range(first, last)])


def around(value, move, count=4):
    return [value] + [move(value, d) for d in range(1, count)]


def deliver(parts, move):
    return [parts[0]] + [move(part, d) for d, part in enumerate(parts) if d > 0]


def params(*sem):
    return pltpu.CompilerParams(dimension_semantics=sem, vmem_limit_bytes=VMEM_BYTES)


def toeplitz_kernel(filter_ref, tile_ref):
    taps = jnp.concatenate([jnp.zeros((1, BLK), f32), filter_ref[0]], axis=1)
    blocks = taps.shape[1] // BLK - 1
    tile_ref[0, 0, BLK:, :BLK] = jnp.zeros((BLK, BLK), bf16)
    for e in range(blocks):
        window = jnp.broadcast_to(taps[:, BLK * e : BLK * (e + 2)], (BLK, 2 * BLK))
        rolled = pltpu.roll(window, 0, 1, stride=1, stride_axis=0)
        piece = rolled[:, BLK:].astype(bf16)
        if e % 2 == 0:
            tile_ref[0, e // 2, :BLK, :BLK] = piece
            tile_ref[0, e // 2, BLK:, BLK:] = piece
        else:
            tile_ref[0, e // 2, :BLK, BLK:] = piece
            if e + 1 < blocks:
                tile_ref[0, e // 2 + 1, BLK:, :BLK] = piece


def toeplitz_tiles(long_filter):
    groups, length = long_filter.shape
    tiles = length // (2 * BLK)
    return pl.pallas_call(
        toeplitz_kernel,
        grid=(groups,),
        in_specs=[pl.BlockSpec((1, 1, length), lambda g: (g, 0, 0))],
        out_specs=pl.BlockSpec((1, tiles, 2 * BLK, 2 * BLK), lambda g: (g, 0, 0, 0)),
        out_shape=jax.ShapeDtypeStruct((groups, tiles, 2 * BLK, 2 * BLK), bf16),
        compiler_params=params("arbitrary"),
        cost_estimate=pl.CostEstimate(flops=8_000_000, bytes_accessed=4_300_000, transcendentals=0),
        name="toeplitz_tiles",
    )(long_filter[:, None, :])


def spread_taps(taps_ref, stream, block):
    groups = taps_ref.shape[2]
    rows = lax.broadcasted_iota(jnp.int32, (groups, CB), 0)
    cols = lax.broadcasted_iota(jnp.int32, (groups, CB), 1)
    spread = (rows == ((block * CB + cols) >> 4)).astype(f32)
    return jnp.dot(
        taps_ref[stream], spread, precision=lax.Precision.HIGHEST, preferred_element_type=f32
    )


def to_channels(value):
    return value.T.reshape(CB // (2 * GROUP), 2, GROUP, BLK).astype(bf16)


def to_positions(value):
    return value.astype(f32).reshape(CB, BLK).T


def featurize_kernel(taps_ref, halo_ref, q_ref, k_ref, v_ref, prod_ref, qf_ref, kf_ref, vf_ref):
    spread = [spread_taps(taps_ref, i, pl.program_id(0)) for i in range(3)]
    for b in range(2):
        feats = []
        for i, (src, dst) in enumerate(((q_ref, qf_ref), (k_ref, kf_ref), (v_ref, vf_ref))):
            ext = jnp.concatenate([halo_ref[i, b].astype(f32), src[b].astype(f32)], axis=0)
            taps = spread[i]
            total = taps[:1] * ext[HALO:]
            for j in range(1, TAPS):
                total = total + taps[j : j + 1] * ext[HALO - j : HALO - j + BLK]
            dst[b] = total
            feats.append(total)
        prod_ref[:, :, b] = to_channels(feats[1] * feats[2])


chan_spec = pl.BlockSpec((CB // (2 * GROUP), 2, 2, GROUP, BLK), lambda c: (c, 0, 0, 0, 0))
pos_spec = pl.BlockSpec((2, BLK, CB), lambda c: (0, 0, c))
taps_spec = pl.BlockSpec((3, TAPS, 64), lambda c: (0, 0, 0))
halo_spec = pl.BlockSpec((3, 2, HALO, CB), lambda c: (0, 0, 0, c))


def chan_shape():
    return jax.ShapeDtypeStruct((NCTX, 2, 2, GROUP, BLK), bf16)


def pos_shape(kind):
    return jax.ShapeDtypeStruct((2, BLK, 1024), kind)


def featurize(taps, halo, q, k, v):
    return pl.pallas_call(
        featurize_kernel,
        grid=(1024 // CB,),
        in_specs=[taps_spec, halo_spec, pos_spec, pos_spec, pos_spec],
        out_specs=[chan_spec, pos_spec, pos_spec, pos_spec],
        out_shape=[chan_shape(), pos_shape(f32), pos_shape(f32), pos_shape(f32)],
        compiler_params=pltpu.CompilerParams(vmem_limit_bytes=62 * 1024 * 1024),
        cost_estimate=pl.CostEstimate(flops=12_000_000, bytes_accessed=5_500_000, transcendentals=0),
        name="featurize",
    )(taps, halo, q, k, v)


def fold(src_ref, dst_ref):
    for i in range(NCTX // 2):
        dst_ref[32 * i : 32 * i + 32, :BLK] = src_ref[2 * i, 0].reshape(32, BLK)
        dst_ref[32 * i : 32 * i + 32, BLK:] = src_ref[2 * i + 1, 0].reshape(32, BLK)


def unfold(acc_ref, dst_ref):
    for i in range(NCTX // 2):
        rows = acc_ref[32 * i : 32 * i + 32].astype(bf16)
        dst_ref[2 * i, 0] = rows[:, :BLK].reshape(2, GROUP, BLK)
        dst_ref[2 * i + 1, 0] = rows[:, BLK:].reshape(2, GROUP, BLK)


def conv_kernel(x_ref, tile_ref, out_ref, x_s, acc_s):
    fold(x_ref, x_s)
    rows = x_s.shape[0]
    for d in range(rows // 32):
        term = jnp.dot(x_s[: rows - 32 * d], tile_ref[0, d], preferred_element_type=f32)
        if d == 0:
            acc_s[...] = term
        else:
            acc_s[32 * d :] += term
    unfold(acc_s, out_ref)


def corr_kernel(x_ref, tile_ref, out_ref, x_s, acc_s):
    fold(x_ref, x_s)
    rows = x_s.shape[0]
    for d in range(rows // 32):
        term = lax.dot_general(
            x_s[32 * d :], tile_ref[0, d], (((1,), (1,)), ((), ())), preferred_element_type=f32
        )
        if d == 0:
            acc_s[...] = term
        else:
            acc_s[: rows - 32 * d] += term
    unfold(acc_s, out_ref)


group_spec = pl.BlockSpec((NCTX, 1, 2, GROUP, BLK), lambda g: (0, g, 0, 0, 0))
tile_spec = pl.BlockSpec((1, 16, 2 * BLK, 2 * BLK), lambda g: (g, 0, 0, 0))


def convolve(kernel, name, x, tiles):
    return pl.pallas_call(
        kernel,
        grid=(2,),
        in_specs=[group_spec, tile_spec],
        out_specs=group_spec,
        out_shape=chan_shape(),
        scratch_shapes=[pltpu.VMEM((512, 256), bf16), pltpu.VMEM((512, 256), f32)],
        compiler_params=params("arbitrary"),
        cost_estimate=pl.CostEstimate(flops=1_100_000_000, bytes_accessed=5_300_000, transcendentals=0),
        name=name,
    )(x, tiles)


def grad_long_kernel(scale, p_ref, g_ref, out_ref, p_s, g_s):
    fold(p_ref, p_s)
    fold(g_ref, g_s)
    g_s[512:] = jnp.zeros((512, 256), bf16)
    rows = lax.broadcasted_iota(jnp.int32, (256, 256), 0)
    cols = lax.broadcasted_iota(jnp.int32, (256, 256), 1)
    flip = (rows + cols == 255).astype(bf16)
    back = lax.dot_general(
        flip, p_s[...], (((1,), (1,)), ((), ())), preferred_element_type=f32
    ).astype(bf16)

    def diagonals(block):
        padded = jnp.concatenate([block, jnp.zeros((BLK, BLK), f32)], axis=1)
        rolled = pltpu.roll(padded, 1, 1, stride=1, stride_axis=0)
        return jnp.sum(rolled, axis=0, keepdims=True)

    def gram(d):
        return jnp.dot(back, g_s[32 * d : 32 * d + 512], preferred_element_type=f32)

    here = gram(0)
    lag = diagonals(here[BLK:, :BLK] + here[:BLK, BLK:])
    for d in range(16):
        later = gram(d + 1) if d < 15 else None
        cross = here[BLK:, BLK:]
        if later is not None:
            cross = cross + later[:BLK, :BLK]
        odd = diagonals(cross)
        out_ref[0, :, 256 * d : 256 * d + BLK] = scale * (lag[:, BLK:] + odd[:, :BLK])
        if later is not None:
            lag = diagonals(later[BLK:, :BLK] + later[:BLK, BLK:])
            out_ref[0, :, 256 * d + BLK : 256 * d + 256] = scale * (odd[:, BLK:] + lag[:, :BLK])
        else:
            out_ref[0, :, 256 * d + BLK : 256 * d + 256] = scale * odd[:, BLK:]
        here = later


def grad_long_call(scale, prod, grad_conv):
    return pl.pallas_call(
        functools.partial(grad_long_kernel, scale),
        grid=(2,),
        in_specs=[group_spec, group_spec],
        out_specs=pl.BlockSpec((1, 1, NCTX * BLK), lambda g: (g, 0, 0)),
        out_shape=jax.ShapeDtypeStruct((2, 1, NCTX * BLK), f32),
        scratch_shapes=[pltpu.VMEM((512, 256), bf16), pltpu.VMEM((1024, 256), bf16)],
        compiler_params=params("arbitrary"),
        cost_estimate=pl.CostEstimate(flops=2_200_000_000, bytes_accessed=1_200_000, transcendentals=0),
        name="grad_long",
    )(prod, grad_conv)[:, 0]


def gate_kernel(conv_ref, qf_ref, gated_ref, convp_ref):
    for b in range(2):
        conv = to_positions(conv_ref[:, :, b])
        convp_ref[b] = conv.astype(bf16)
        gated_ref[b] = (qf_ref[b] * conv).astype(bf16)


def gate(conv, qf):
    return pl.pallas_call(
        gate_kernel,
        grid=(1024 // CB,),
        in_specs=[chan_spec, pos_spec],
        out_specs=[pos_spec, pos_spec],
        out_shape=[pos_shape(bf16), pos_shape(bf16)],
        compiler_params=params("arbitrary"),
        cost_estimate=pl.CostEstimate(flops=1_000_000, bytes_accessed=2_500_000, transcendentals=0),
        name="gate",
    )(conv, qf)


def grad_conv_kernel(own_ref, other_ref, qf_ref, gc_ref, gg_ref):
    for b in range(2):
        total = own_ref[b] + other_ref[b].astype(f32)
        gg_ref[b] = total
        gc_ref[:, :, b] = to_channels(total * qf_ref[b])


def grad_conv_call(own, other, qf):
    return pl.pallas_call(
        grad_conv_kernel,
        grid=(1024 // CB,),
        in_specs=[pos_spec, pos_spec, pos_spec],
        out_specs=[chan_spec, pos_spec],
        out_shape=[chan_shape(), pos_shape(f32)],
        compiler_params=params("arbitrary"),
        cost_estimate=pl.CostEstimate(flops=1_000_000, bytes_accessed=4_000_000, transcendentals=0),
        name="grad_conv",
    )(own, other, qf)


def unpack_kernel(gp_ref, kf_ref, vf_ref, gpp_ref, first_ref):
    for b in range(2):
        grad = to_positions(gp_ref[:, :, b])
        gpp_ref[b] = grad.astype(bf16)
        first_ref[0, b] = (grad[:HALO] * vf_ref[b]).astype(bf16)
        first_ref[1, b] = (grad[:HALO] * kf_ref[b]).astype(bf16)


def unpack(gp, kf, vf):
    rows_spec = pl.BlockSpec((2, HALO, CB), lambda c: (0, 0, c))
    return pl.pallas_call(
        unpack_kernel,
        grid=(1024 // CB,),
        in_specs=[chan_spec, rows_spec, rows_spec],
        out_specs=[pos_spec, pl.BlockSpec((2, 2, HALO, CB), lambda c: (0, 0, 0, c))],
        out_shape=[pos_shape(bf16), jax.ShapeDtypeStruct((2, 2, HALO, 1024), bf16)],
        compiler_params=params("arbitrary"),
        cost_estimate=pl.CostEstimate(flops=500_000, bytes_accessed=1_200_000, transcendentals=0),
        name="unpack",
    )(gp, kf, vf)


def backward_taps(grad, halo, taps):
    ext = jnp.concatenate([grad, halo.astype(f32)], axis=0)
    total = taps[:1] * grad
    for j in range(1, TAPS):
        total = total + taps[j : j + 1] * ext[j : j + BLK]
    return total.astype(bf16)


def grad_query_kernel(taps_ref, halo_ref, gg_ref, conv_ref, out_ref):
    taps = spread_taps(taps_ref, 0, pl.program_id(0))
    for b in range(2):
        out_ref[b] = backward_taps(gg_ref[b] * conv_ref[b].astype(f32), halo_ref[0, b], taps)


def grad_query_call(taps, halo, gg, conv):
    return pl.pallas_call(
        grad_query_kernel,
        grid=(1024 // CB,),
        in_specs=[
            taps_spec,
            pl.BlockSpec((1, 2, HALO, CB), lambda c: (0, 0, 0, c)),
            pos_spec,
            pos_spec,
        ],
        out_specs=pos_spec,
        out_shape=pos_shape(bf16),
        compiler_params=params("arbitrary"),
        cost_estimate=pl.CostEstimate(flops=4_000_000, bytes_accessed=2_100_000, transcendentals=0),
        name="grad_query",
    )(taps, halo, gg, conv)


def grad_kv_kernel(taps_ref, halo_ref, gp_ref, kf_ref, vf_ref, gk_ref, gv_ref):
    key_taps = spread_taps(taps_ref, 1, pl.program_id(0))
    value_taps = spread_taps(taps_ref, 2, pl.program_id(0))
    for b in range(2):
        grad = gp_ref[b].astype(f32)
        gk_ref[b] = backward_taps(grad * vf_ref[b], halo_ref[0, b], key_taps)
        gv_ref[b] = backward_taps(grad * kf_ref[b], halo_ref[1, b], value_taps)


def grad_kv_call(taps, halo, gp, kf, vf):
    return pl.pallas_call(
        grad_kv_kernel,
        grid=(1024 // CB,),
        in_specs=[
            taps_spec,
            pl.BlockSpec((2, 2, HALO, CB), lambda c: (0, 0, 0, c)),
            pos_spec,
            pos_spec,
            pos_spec,
        ],
        out_specs=[pos_spec, pos_spec],
        out_shape=[pos_shape(bf16), pos_shape(bf16)],
        compiler_params=params("arbitrary"),
        cost_estimate=pl.CostEstimate(flops=8_000_000, bytes_accessed=4_000_000, transcendentals=0),
        name="grad_kv",
    )(taps, halo, gp, kf, vf)


def vmem(count=1):
    return [pl.BlockSpec(memory_space=pltpu.VMEM)] * count


smem = pl.BlockSpec(memory_space=pltpu.SMEM)


def whole(kernel, name, ins, outs, flops=0, scratch=(), index=True):
    size = sum(a.size * a.dtype.itemsize for a in ins)
    size += sum(a.size * jnp.dtype(a.dtype).itemsize for a in outs)
    return pl.pallas_call(
        kernel,
        in_specs=([smem] if index else []) + vmem(len(ins) - int(index)),
        out_specs=vmem(len(outs)),
        out_shape=list(outs),
        scratch_shapes=list(scratch),
        compiler_params=pltpu.CompilerParams(vmem_limit_bytes=VMEM_BYTES),
        cost_estimate=pl.CostEstimate(flops=flops, bytes_accessed=size, transcendentals=0),
        name=name,
    )(*ins)


def shape(dims, kind=bf16):
    return jax.ShapeDtypeStruct(dims, kind)


def prep_kernel(at, q_ref, k_ref, v_ref, g_ref, last_ref, mine_ref, theirs_ref):
    first_core = at[3] == 0
    for i, src in enumerate((q_ref, k_ref, v_ref)):
        last_ref[i] = src[...]
    for x in range(NX):
        lo = g_ref[:, 256 * x : 256 * x + BLK]
        hi = g_ref[:, 256 * x + BLK : 256 * x + 256]
        mine_ref[:, BLK * x : BLK * x + BLK] = jnp.where(first_core, lo, hi)
        theirs_ref[:, BLK * x : BLK * x + BLK] = jnp.where(first_core, hi, lo)


def prep(at, q, k, v, grad_out):
    rows = pl.BlockSpec((2, HALO, 1024), lambda i: (0, BLK // HALO - 1, 0))
    full = lambda dims: pl.BlockSpec(dims, lambda i: (0,) * len(dims))
    return pl.pallas_call(
        prep_kernel,
        grid=(1,),
        in_specs=[smem, rows, rows, rows, full((256, 1024))],
        out_specs=[full((3, 2, HALO, 1024)), full((256, 512)), full((256, 512))],
        out_shape=[
            shape((3, 2, HALO, 1024)),
            shape((256, 512)),
            shape((256, 512)),
        ],
        compiler_params=pltpu.CompilerParams(vmem_limit_bytes=62 * 1024 * 1024),
        name="prep",
    )(at, q, k, v, grad_out)


def grad_gated_kernel(at, c0, c1, c2, c3, w_ref, own_ref, other_ref):
    total = jnp.zeros((512, 256), f32)
    for d, cols in enumerate((c0, c1, c2, c3)):
        total = total + jnp.dot(
            cols[...], w_ref[(at[2] + 4 - d) & 3], preferred_element_type=f32
        )
    own_ref[...] = total[:256]
    other_ref[...] = total[256:].astype(bf16)


def grad_gated_call(at, columns, weights):
    fixed = pl.BlockSpec((512, 512), lambda n: (0, 0))
    return pl.pallas_call(
        grad_gated_kernel,
        grid=(4,),
        in_specs=[smem] + [fixed] * 4 + [pl.BlockSpec((4, 512, 256), lambda n: (0, 0, n))],
        out_specs=[pl.BlockSpec((256, 256), lambda n: (0, n))] * 2,
        out_shape=[shape((256, 1024), f32), shape((256, 1024))],
        compiler_params=params("arbitrary"),
        cost_estimate=pl.CostEstimate(flops=2_200_000_000, bytes_accessed=7_800_000, transcendentals=0),
        name="grad_gated",
    )(at, *columns, weights)


def mixed_kernel(at, own_g, other_g, w_ref, *outs):
    for d in range(4):
        block = w_ref[(at[2] + d) & 3]
        for i, src in enumerate((own_g, other_g)):
            part = lax.dot_general(
                src[...], block, (((1,), (1,)), ((), ())), preferred_element_type=f32
            )
            outs[d][256 * i : 256 * i + 256] = part.astype(outs[d].dtype)


def mixed_call(at, own, other, weights):
    fixed = pl.BlockSpec((256, 1024), lambda n: (0, 0))
    return pl.pallas_call(
        mixed_kernel,
        grid=(2,),
        in_specs=[smem, fixed, fixed, pl.BlockSpec((4, 256, 1024), lambda n: (0, n, 0))],
        out_specs=[pl.BlockSpec((512, 256), lambda n: (0, n))] * 4,
        out_shape=[shape((512, 512), f32)] + [shape((512, 512))] * 3,
        compiler_params=params("arbitrary"),
        cost_estimate=pl.CostEstimate(flops=2_200_000_000, bytes_accessed=7_800_000, transcendentals=0),
        name="mixed",
    )(at, own, other, weights)


def mixed_sum_kernel(own, a_ref, b_ref, c_ref, keep_ref, send_ref):
    total = own[...] + a_ref[...].astype(f32) + b_ref[...].astype(f32) + c_ref[...].astype(f32)
    keep_ref[...] = total[:256].astype(bf16)
    send_ref[...] = total[256:].astype(bf16)


def mixed_out_kernel(at, keep_ref, came_ref, out_ref):
    first_core = at[3] == 0
    for x in range(NX):
        keep = keep_ref[:, BLK * x : BLK * x + BLK]
        came = came_ref[:, BLK * x : BLK * x + BLK]
        out_ref[:, 256 * x : 256 * x + BLK] = jnp.where(first_core, keep, came)
        out_ref[:, 256 * x + BLK : 256 * x + 256] = jnp.where(first_core, came, keep)


def weight_grad_kernel(at, c0, c1, c2, c3, own_g, other_g, out_ref):
    for d, cols in enumerate((c0, c1, c2, c3)):
        total = 0.0
        for i, src in enumerate((own_g, other_g)):
            total = total + lax.dot_general(
                cols[256 * i : 256 * i + 256],
                src[...],
                (((0,), (0,)), ((), ())),
                preferred_element_type=f32,
            )
        out_ref[(at[2] + 4 - d) & 3] = total.astype(bf16)


def weight_grad_call(at, columns, own, other):
    fixed = pl.BlockSpec((512, 512), lambda n: (0, 0))
    return pl.pallas_call(
        weight_grad_kernel,
        grid=(2,),
        in_specs=[smem] + [fixed] * 4 + [pl.BlockSpec((256, 512), lambda n: (0, n))] * 2,
        out_specs=pl.BlockSpec((4, 512, 512), lambda n: (0, 0, n)),
        out_shape=shape((4, 512, 1024)),
        compiler_params=params("arbitrary"),
        cost_estimate=pl.CostEstimate(flops=2_200_000_000, bytes_accessed=7_800_000, transcendentals=0),
        name="grad_weight",
    )(at, *columns, own, other)


def exchange(value):
    return lax.all_to_all(value, "context", split_axis=0, concat_axis=0, tiled=True)


def body(query_in, key_in, value_in, short_filter, long_filter, out_weight, grad_out):
    batches, rows, channels = query_in.shape
    scale = float(batches * rows * NCTX * GROUP) ** (-0.5)
    ctx = lax.axis_index("context")
    at_y = lax.axis_index("tensor")
    at = jnp.stack([ctx // (NC * NX), (ctx // NC) % NX, at_y, ctx % NC]).astype(jnp.int32)
    positions = batches * rows
    half = channels // 2

    taps = short_filter
    same_core = [list(range(c, NCTX, NC)) for c in range(NC)]
    weights = lax.all_gather(
        out_weight,
        "context",
        axis=0,
        tiled=True,
        axis_index_groups=same_core,
    ).reshape(NY, half, channels)
    last, mine, theirs = prep(
        at, query_in, key_in, value_in, grad_out.reshape(positions, channels)
    )
    before = next_context(last, 1)

    columns = jnp.concatenate([mine, swap_core(theirs)])
    columns, before = lax.optimization_barrier((columns, before))
    columns = around(columns, move_y)

    tiles = toeplitz_tiles(long_filter)
    prod, qf, kf, vf = featurize(taps, before, query_in, key_in, value_in)
    prod = exchange(prod)
    prod, *columns = lax.optimization_barrier((prod, *columns))
    conv = exchange(convolve(conv_kernel, "conv", prod, tiles))
    gated, conv = gate(conv, qf)
    gated_own = gated.reshape(positions, channels)
    gated_other = swap_core(gated_own)

    sums = weight_grad_call(at, columns, gated_own, gated_other).reshape(-1, channels)
    weights, sums = lax.optimization_barrier((weights, sums))
    own, other = grad_gated_call(at, columns, weights)
    other = swap_core(other)
    grad_conv, grad_gated = grad_conv_call(
        own.reshape(query_in.shape), other.reshape(query_in.shape), qf
    )
    grad_conv, gated_late = lax.optimization_barrier((grad_conv, gated_own))
    grad_conv_all = exchange(grad_conv)

    grad_weight = lax.psum_scatter(
        sums, "context", scatter_dimension=0, axis_index_groups=same_core, tiled=True
    ).astype(f32)

    mixed = mixed_call(at, gated_late, gated_other, weights)
    mixed = deliver(mixed, move_y)
    keep, send = whole(
        mixed_sum_kernel, "mixed_sum", mixed, [shape((positions, half))] * 2, index=False
    )
    (mixed_out,) = whole(
        mixed_out_kernel, "mixed_out", [at, keep, swap_core(send)], [shape((positions, channels))]
    )
    mixed_out = mixed_out.reshape(query_in.shape)
    first_q = (grad_gated[:, :HALO] * conv[:, :HALO].astype(f32)).astype(bf16)[None]
    after_q = next_context(first_q, -1)
    grad_query = grad_query_call(taps, after_q, grad_gated, conv)

    grad_product = exchange(convolve(corr_kernel, "corr", grad_conv_all, tiles))
    grad_long = grad_long_call(scale, prod, grad_conv_all)
    grad_product, grad_long, grad_query = lax.optimization_barrier(
        (grad_product, grad_long, grad_query)
    )
    grad_product, first_kv = unpack(grad_product, kf, vf)
    after_kv = next_context(first_kv, -1)
    grad_key, grad_value = grad_kv_call(taps, after_kv, grad_product, kf, vf)
    return (mixed_out, grad_query, grad_key, grad_value, grad_weight, grad_long)


def solution(mesh):
    act = P(None, "context", "tensor")
    in_specs = (
        act,
        act,
        act,
        P(None, None, "tensor"),
        P(("tensor", "context"), None),
        P("context", "tensor"),
        act,
    )
    out_specs = (act, act, act, act, P("context", "tensor"), P(("tensor", "context"), None))
    return jax.shard_map(body, mesh=mesh, in_specs=in_specs, out_specs=out_specs, check_vma=False)
```

```python
import functools

import jax
import jax.numpy as jnp
from jax import lax
from jax.experimental import pallas as pl
from jax.experimental.pallas import tpu as pltpu
from jax.sharding import PartitionSpec as P

GROUP = 16
TAPS = 7
HALO = 16
NZ, NX, NC, NY = 4, 4, 2, 4
NCTX = NZ * NX * NC
BLK = 128
CB = 256
VMEM_BYTES = 48 * 1024 * 1024
f32 = jnp.float32
bf16 = jnp.bfloat16


def move_ctx(value, dz, dx, dc):
    pairs = []
    for z in range(NZ):
        for x in range(NX):
            for c in range(NC):
                src = (z * NX + x) * NC + c
                dst = (((z + dz) % NZ) * NX + (x + dx) % NX) * NC + (c + dc) % NC
                pairs.append((src, dst))
    return lax.ppermute(value, "context", pairs)


def move_z(value, d):
    return move_ctx(value, d, 0, 0)


def move_x(value, d):
    return move_ctx(value, 0, d, 0)


def swap_core(value):
    return move_ctx(value, 0, 0, 1)


def move_y(value, d):
    return lax.ppermute(value, "tensor", [(i, (i + d) % NY) for i in range(NY)])


def next_context(value, steps):
    first, last = (max(0, -steps), min(NCTX, NCTX - steps))
    return lax.ppermute(value, "context", [(s, s + steps) for s in range(first, last)])


def around(value, move, count=4):
    return [value] + [move(value, d) for d in range(1, count)]


def deliver(parts, move):
    return [parts[0]] + [move(part, d) for d, part in enumerate(parts) if d > 0]


def params(*sem):
    return pltpu.CompilerParams(dimension_semantics=sem, vmem_limit_bytes=VMEM_BYTES)


def toeplitz_kernel(filter_ref, tile_ref):
    taps = jnp.concatenate([jnp.zeros((1, BLK), f32), filter_ref[0]], axis=1)
    blocks = taps.shape[1] // BLK - 1
    tile_ref[0, 0, BLK:, :BLK] = jnp.zeros((BLK, BLK), bf16)
    for e in range(blocks):
        window = jnp.broadcast_to(taps[:, BLK * e : BLK * (e + 2)], (BLK, 2 * BLK))
        rolled = pltpu.roll(window, 0, 1, stride=1, stride_axis=0)
        piece = rolled[:, BLK:].astype(bf16)
        if e % 2 == 0:
            tile_ref[0, e // 2, :BLK, :BLK] = piece
            tile_ref[0, e // 2, BLK:, BLK:] = piece
        else:
            tile_ref[0, e // 2, :BLK, BLK:] = piece
            if e + 1 < blocks:
                tile_ref[0, e // 2 + 1, BLK:, :BLK] = piece


def toeplitz_tiles(long_filter):
    groups, length = long_filter.shape
    tiles = length // (2 * BLK)
    return pl.pallas_call(
        toeplitz_kernel,
        grid=(groups,),
        in_specs=[pl.BlockSpec((1, 1, length), lambda g: (g, 0, 0))],
        out_specs=pl.BlockSpec((1, tiles, 2 * BLK, 2 * BLK), lambda g: (g, 0, 0, 0)),
        out_shape=jax.ShapeDtypeStruct((groups, tiles, 2 * BLK, 2 * BLK), bf16),
        compiler_params=params("arbitrary"),
        cost_estimate=pl.CostEstimate(flops=8_000_000, bytes_accessed=4_300_000, transcendentals=0),
        name="toeplitz_tiles",
    )(long_filter[:, None, :])


def spread_taps(taps_ref, stream, block):
    groups = taps_ref.shape[2]
    rows = lax.broadcasted_iota(jnp.int32, (groups, CB), 0)
    cols = lax.broadcasted_iota(jnp.int32, (groups, CB), 1)
    spread = (rows == ((block * CB + cols) >> 4)).astype(f32)
    return jnp.dot(
        taps_ref[stream], spread, precision=lax.Precision.HIGHEST, preferred_element_type=f32
    )


def to_channels(value):
    return value.T.reshape(CB // (2 * GROUP), 2, GROUP, BLK).astype(bf16)


def to_positions(value):
    return value.astype(f32).reshape(CB, BLK).T


def featurize_kernel(taps_ref, halo_ref, q_ref, k_ref, v_ref, prod_ref, qf_ref, kf_ref, vf_ref):
    spread = [spread_taps(taps_ref, i, pl.program_id(0)) for i in range(3)]
    for b in range(2):
        feats = []
        for i, (src, dst) in enumerate(((q_ref, qf_ref), (k_ref, kf_ref), (v_ref, vf_ref))):
            ext = jnp.concatenate([halo_ref[i, b].astype(f32), src[b].astype(f32)], axis=0)
            taps = spread[i]
            total = taps[:1] * ext[HALO:]
            for j in range(1, TAPS):
                total = total + taps[j : j + 1] * ext[HALO - j : HALO - j + BLK]
            dst[b] = total
            feats.append(total)
        prod_ref[:, :, b] = to_channels(feats[1] * feats[2])


chan_spec = pl.BlockSpec((CB // (2 * GROUP), 2, 2, GROUP, BLK), lambda c: (c, 0, 0, 0, 0))
pos_spec = pl.BlockSpec((2, BLK, CB), lambda c: (0, 0, c))
taps_spec = pl.BlockSpec((3, TAPS, 64), lambda c: (0, 0, 0))
halo_spec = pl.BlockSpec((3, 2, HALO, CB), lambda c: (0, 0, 0, c))


def chan_shape():
    return jax.ShapeDtypeStruct((NCTX, 2, 2, GROUP, BLK), bf16)


def pos_shape(kind):
    return jax.ShapeDtypeStruct((2, BLK, 1024), kind)


def featurize(taps, halo, q, k, v):
    return pl.pallas_call(
        featurize_kernel,
        grid=(1024 // CB,),
        in_specs=[taps_spec, halo_spec, pos_spec, pos_spec, pos_spec],
        out_specs=[chan_spec, pos_spec, pos_spec, pos_spec],
        out_shape=[chan_shape(), pos_shape(f32), pos_shape(f32), pos_shape(f32)],
        compiler_params=pltpu.CompilerParams(vmem_limit_bytes=62 * 1024 * 1024),
        cost_estimate=pl.CostEstimate(flops=12_000_000, bytes_accessed=5_500_000, transcendentals=0),
        name="featurize",
    )(taps, halo, q, k, v)


def fold(src_ref, dst_ref):
    for i in range(NCTX // 2):
        dst_ref[32 * i : 32 * i + 32, :BLK] = src_ref[2 * i, 0].reshape(32, BLK)
        dst_ref[32 * i : 32 * i + 32, BLK:] = src_ref[2 * i + 1, 0].reshape(32, BLK)


def unfold(acc_ref, dst_ref):
    for i in range(NCTX // 2):
        rows = acc_ref[32 * i : 32 * i + 32].astype(bf16)
        dst_ref[2 * i, 0] = rows[:, :BLK].reshape(2, GROUP, BLK)
        dst_ref[2 * i + 1, 0] = rows[:, BLK:].reshape(2, GROUP, BLK)


def conv_kernel(x_ref, tile_ref, out_ref, x_s, acc_s):
    fold(x_ref, x_s)
    rows = x_s.shape[0]
    for d in range(rows // 32):
        term = jnp.dot(x_s[: rows - 32 * d], tile_ref[0, d], preferred_element_type=f32)
        if d == 0:
            acc_s[...] = term
        else:
            acc_s[32 * d :] += term
    unfold(acc_s, out_ref)


def corr_kernel(x_ref, tile_ref, out_ref, x_s, acc_s):
    fold(x_ref, x_s)
    rows = x_s.shape[0]
    for d in range(rows // 32):
        term = lax.dot_general(
            x_s[32 * d :], tile_ref[0, d], (((1,), (1,)), ((), ())), preferred_element_type=f32
        )
        if d == 0:
            acc_s[...] = term
        else:
            acc_s[: rows - 32 * d] += term
    unfold(acc_s, out_ref)


group_spec = pl.BlockSpec((NCTX, 1, 2, GROUP, BLK), lambda g: (0, g, 0, 0, 0))
tile_spec = pl.BlockSpec((1, 16, 2 * BLK, 2 * BLK), lambda g: (g, 0, 0, 0))


def convolve(kernel, name, x, tiles):
    return pl.pallas_call(
        kernel,
        grid=(2,),
        in_specs=[group_spec, tile_spec],
        out_specs=group_spec,
        out_shape=chan_shape(),
        scratch_shapes=[pltpu.VMEM((512, 256), bf16), pltpu.VMEM((512, 256), f32)],
        compiler_params=params("arbitrary"),
        cost_estimate=pl.CostEstimate(flops=1_100_000_000, bytes_accessed=5_300_000, transcendentals=0),
        name=name,
    )(x, tiles)


def grad_long_kernel(scale, p_ref, g_ref, out_ref, p_s, g_s):
    fold(p_ref, p_s)
    fold(g_ref, g_s)
    g_s[512:] = jnp.zeros((512, 256), bf16)
    rows = lax.broadcasted_iota(jnp.int32, (256, 256), 0)
    cols = lax.broadcasted_iota(jnp.int32, (256, 256), 1)
    flip = (rows + cols == 255).astype(bf16)
    back = lax.dot_general(
        flip, p_s[...], (((1,), (1,)), ((), ())), preferred_element_type=f32
    ).astype(bf16)

    def diagonals(block):
        padded = jnp.concatenate([block, jnp.zeros((BLK, BLK), f32)], axis=1)
        rolled = pltpu.roll(padded, 1, 1, stride=1, stride_axis=0)
        return jnp.sum(rolled, axis=0, keepdims=True)

    def gram(d):
        return jnp.dot(back, g_s[32 * d : 32 * d + 512], preferred_element_type=f32)

    here = gram(0)
    lag = diagonals(here[BLK:, :BLK] + here[:BLK, BLK:])
    for d in range(16):
        later = gram(d + 1) if d < 15 else None
        cross = here[BLK:, BLK:]
        if later is not None:
            cross = cross + later[:BLK, :BLK]
        odd = diagonals(cross)
        out_ref[0, :, 256 * d : 256 * d + BLK] = scale * (lag[:, BLK:] + odd[:, :BLK])
        if later is not None:
            lag = diagonals(later[BLK:, :BLK] + later[:BLK, BLK:])
            out_ref[0, :, 256 * d + BLK : 256 * d + 256] = scale * (odd[:, BLK:] + lag[:, :BLK])
        else:
            out_ref[0, :, 256 * d + BLK : 256 * d + 256] = scale * odd[:, BLK:]
        here = later


def grad_long_call(scale, prod, grad_conv):
    return pl.pallas_call(
        functools.partial(grad_long_kernel, scale),
        grid=(2,),
        in_specs=[group_spec, group_spec],
        out_specs=pl.BlockSpec((1, 1, NCTX * BLK), lambda g: (g, 0, 0)),
        out_shape=jax.ShapeDtypeStruct((2, 1, NCTX * BLK), f32),
        scratch_shapes=[pltpu.VMEM((512, 256), bf16), pltpu.VMEM((1024, 256), bf16)],
        compiler_params=params("arbitrary"),
        cost_estimate=pl.CostEstimate(flops=2_200_000_000, bytes_accessed=1_200_000, transcendentals=0),
        name="grad_long",
    )(prod, grad_conv)[:, 0]


def gate_kernel(conv_ref, qf_ref, gated_ref, convp_ref):
    for b in range(2):
        conv = to_positions(conv_ref[:, :, b])
        convp_ref[b] = conv.astype(bf16)
        gated_ref[b] = (qf_ref[b] * conv).astype(bf16)


def gate(conv, qf):
    return pl.pallas_call(
        gate_kernel,
        grid=(1024 // CB,),
        in_specs=[chan_spec, pos_spec],
        out_specs=[pos_spec, pos_spec],
        out_shape=[pos_shape(bf16), pos_shape(bf16)],
        compiler_params=params("arbitrary"),
        cost_estimate=pl.CostEstimate(flops=1_000_000, bytes_accessed=2_500_000, transcendentals=0),
        name="gate",
    )(conv, qf)


def grad_conv_kernel(own_ref, other_ref, qf_ref, gc_ref, gg_ref):
    for b in range(2):
        total = own_ref[b] + other_ref[b].astype(f32)
        gg_ref[b] = total
        gc_ref[:, :, b] = to_channels(total * qf_ref[b])


def grad_conv_call(own, other, qf):
    return pl.pallas_call(
        grad_conv_kernel,
        grid=(1024 // CB,),
        in_specs=[pos_spec, pos_spec, pos_spec],
        out_specs=[chan_spec, pos_spec],
        out_shape=[chan_shape(), pos_shape(f32)],
        compiler_params=params("arbitrary"),
        cost_estimate=pl.CostEstimate(flops=1_000_000, bytes_accessed=4_000_000, transcendentals=0),
        name="grad_conv",
    )(own, other, qf)


def unpack_kernel(gp_ref, kf_ref, vf_ref, gpp_ref, first_ref):
    for b in range(2):
        grad = to_positions(gp_ref[:, :, b])
        gpp_ref[b] = grad.astype(bf16)
        first_ref[0, b] = (grad[:HALO] * vf_ref[b]).astype(bf16)
        first_ref[1, b] = (grad[:HALO] * kf_ref[b]).astype(bf16)


def unpack(gp, kf, vf):
    rows_spec = pl.BlockSpec((2, HALO, CB), lambda c: (0, 0, c))
    return pl.pallas_call(
        unpack_kernel,
        grid=(1024 // CB,),
        in_specs=[chan_spec, rows_spec, rows_spec],
        out_specs=[pos_spec, pl.BlockSpec((2, 2, HALO, CB), lambda c: (0, 0, 0, c))],
        out_shape=[pos_shape(bf16), jax.ShapeDtypeStruct((2, 2, HALO, 1024), bf16)],
        compiler_params=params("arbitrary"),
        cost_estimate=pl.CostEstimate(flops=500_000, bytes_accessed=1_200_000, transcendentals=0),
        name="unpack",
    )(gp, kf, vf)


def backward_taps(grad, halo, taps):
    ext = jnp.concatenate([grad, halo.astype(f32)], axis=0)
    total = taps[:1] * grad
    for j in range(1, TAPS):
        total = total + taps[j : j + 1] * ext[j : j + BLK]
    return total.astype(bf16)


def grad_query_kernel(taps_ref, halo_ref, gg_ref, conv_ref, out_ref):
    taps = spread_taps(taps_ref, 0, pl.program_id(0))
    for b in range(2):
        out_ref[b] = backward_taps(gg_ref[b] * conv_ref[b].astype(f32), halo_ref[0, b], taps)


def grad_query_call(taps, halo, gg, conv):
    return pl.pallas_call(
        grad_query_kernel,
        grid=(1024 // CB,),
        in_specs=[
            taps_spec,
            pl.BlockSpec((1, 2, HALO, CB), lambda c: (0, 0, 0, c)),
            pos_spec,
            pos_spec,
        ],
        out_specs=pos_spec,
        out_shape=pos_shape(bf16),
        compiler_params=params("arbitrary"),
        cost_estimate=pl.CostEstimate(flops=4_000_000, bytes_accessed=2_100_000, transcendentals=0),
        name="grad_query",
    )(taps, halo, gg, conv)


def grad_kv_kernel(taps_ref, halo_ref, gp_ref, kf_ref, vf_ref, gk_ref, gv_ref):
    key_taps = spread_taps(taps_ref, 1, pl.program_id(0))
    value_taps = spread_taps(taps_ref, 2, pl.program_id(0))
    for b in range(2):
        grad = gp_ref[b].astype(f32)
        gk_ref[b] = backward_taps(grad * vf_ref[b], halo_ref[0, b], key_taps)
        gv_ref[b] = backward_taps(grad * kf_ref[b], halo_ref[1, b], value_taps)


def grad_kv_call(taps, halo, gp, kf, vf):
    return pl.pallas_call(
        grad_kv_kernel,
        grid=(1024 // CB,),
        in_specs=[
            taps_spec,
            pl.BlockSpec((2, 2, HALO, CB), lambda c: (0, 0, 0, c)),
            pos_spec,
            pos_spec,
            pos_spec,
        ],
        out_specs=[pos_spec, pos_spec],
        out_shape=[pos_shape(bf16), pos_shape(bf16)],
        compiler_params=params("arbitrary"),
        cost_estimate=pl.CostEstimate(flops=8_000_000, bytes_accessed=4_000_000, transcendentals=0),
        name="grad_kv",
    )(taps, halo, gp, kf, vf)


def vmem(count=1):
    return [pl.BlockSpec(memory_space=pltpu.VMEM)] * count


smem = pl.BlockSpec(memory_space=pltpu.SMEM)


def whole(kernel, name, ins, outs, flops=0, scratch=(), index=True):
    size = sum(a.size * a.dtype.itemsize for a in ins)
    size += sum(a.size * jnp.dtype(a.dtype).itemsize for a in outs)
    return pl.pallas_call(
        kernel,
        in_specs=([smem] if index else []) + vmem(len(ins) - int(index)),
        out_specs=vmem(len(outs)),
        out_shape=list(outs),
        scratch_shapes=list(scratch),
        compiler_params=pltpu.CompilerParams(vmem_limit_bytes=VMEM_BYTES),
        cost_estimate=pl.CostEstimate(flops=flops, bytes_accessed=size, transcendentals=0),
        name=name,
    )(*ins)


def shape(dims, kind=bf16):
    return jax.ShapeDtypeStruct(dims, kind)


def prep_kernel(at, q_ref, k_ref, v_ref, g_ref, last_ref, mine_ref, theirs_ref):
    first_core = at[3] == 0
    for i, src in enumerate((q_ref, k_ref, v_ref)):
        last_ref[i] = src[...]
    for x in range(NX):
        lo = g_ref[:, 256 * x : 256 * x + BLK]
        hi = g_ref[:, 256 * x + BLK : 256 * x + 256]
        mine_ref[:, BLK * x : BLK * x + BLK] = jnp.where(first_core, lo, hi)
        theirs_ref[:, BLK * x : BLK * x + BLK] = jnp.where(first_core, hi, lo)


def prep(at, q, k, v, grad_out):
    rows = pl.BlockSpec((2, HALO, 1024), lambda i: (0, BLK // HALO - 1, 0))
    full = lambda dims: pl.BlockSpec(dims, lambda i: (0,) * len(dims))
    return pl.pallas_call(
        prep_kernel,
        grid=(1,),
        in_specs=[smem, rows, rows, rows, full((256, 1024))],
        out_specs=[full((3, 2, HALO, 1024)), full((256, 512)), full((256, 512))],
        out_shape=[
            shape((3, 2, HALO, 1024)),
            shape((256, 512)),
            shape((256, 512)),
        ],
        compiler_params=pltpu.CompilerParams(vmem_limit_bytes=62 * 1024 * 1024),
        name="prep",
    )(at, q, k, v, grad_out)


def grad_gated_kernel(at, c0, c1, c2, c3, w_ref, own_ref, other_ref):
    total = jnp.zeros((512, 256), f32)
    for d, cols in enumerate((c0, c1, c2, c3)):
        total = total + jnp.dot(
            cols[...], w_ref[(at[2] + 4 - d) & 3], preferred_element_type=f32
        )
    own_ref[...] = total[:256]
    other_ref[...] = total[256:].astype(bf16)


def grad_gated_call(at, columns, weights):
    fixed = pl.BlockSpec((512, 512), lambda n: (0, 0))
    return pl.pallas_call(
        grad_gated_kernel,
        grid=(4,),
        in_specs=[smem] + [fixed] * 4 + [pl.BlockSpec((4, 512, 256), lambda n: (0, 0, n))],
        out_specs=[pl.BlockSpec((256, 256), lambda n: (0, n))] * 2,
        out_shape=[shape((256, 1024), f32), shape((256, 1024))],
        compiler_params=params("arbitrary"),
        cost_estimate=pl.CostEstimate(flops=2_200_000_000, bytes_accessed=7_800_000, transcendentals=0),
        name="grad_gated",
    )(at, *columns, weights)


def mixed_kernel(at, own_g, other_g, w_ref, *outs):
    for d in range(4):
        block = w_ref[(at[2] + d) & 3]
        for i, src in enumerate((own_g, other_g)):
            part = lax.dot_general(
                src[...], block, (((1,), (1,)), ((), ())), preferred_element_type=f32
            )
            outs[d][256 * i : 256 * i + 256] = part.astype(outs[d].dtype)


def mixed_call(at, own, other, weights):
    fixed = pl.BlockSpec((256, 1024), lambda n: (0, 0))
    return pl.pallas_call(
        mixed_kernel,
        grid=(2,),
        in_specs=[smem, fixed, fixed, pl.BlockSpec((4, 256, 1024), lambda n: (0, n, 0))],
        out_specs=[pl.BlockSpec((512, 256), lambda n: (0, n))] * 4,
        out_shape=[shape((512, 512), f32)] + [shape((512, 512))] * 3,
        compiler_params=params("arbitrary"),
        cost_estimate=pl.CostEstimate(flops=2_200_000_000, bytes_accessed=7_800_000, transcendentals=0),
        name="mixed",
    )(at, own, other, weights)


def mixed_sum_kernel(own, a_ref, b_ref, c_ref, keep_ref, send_ref):
    total = own[...] + a_ref[...].astype(f32) + b_ref[...].astype(f32) + c_ref[...].astype(f32)
    keep_ref[...] = total[:256].astype(bf16)
    send_ref[...] = total[256:].astype(bf16)


def mixed_out_kernel(at, keep_ref, came_ref, out_ref):
    first_core = at[3] == 0
    for x in range(NX):
        keep = keep_ref[:, BLK * x : BLK * x + BLK]
        came = came_ref[:, BLK * x : BLK * x + BLK]
        out_ref[:, 256 * x : 256 * x + BLK] = jnp.where(first_core, keep, came)
        out_ref[:, 256 * x + BLK : 256 * x + 256] = jnp.where(first_core, came, keep)


def weight_grad_kernel(at, c0, c1, c2, c3, own_g, other_g, out_ref):
    for d, cols in enumerate((c0, c1, c2, c3)):
        total = 0.0
        for i, src in enumerate((own_g, other_g)):
            total = total + lax.dot_general(
                cols[256 * i : 256 * i + 256],
                src[...],
                (((0,), (0,)), ((), ())),
                preferred_element_type=f32,
            )
        out_ref[(at[2] + 4 - d) & 3] = total.astype(bf16)


def weight_grad_call(at, columns, own, other):
    fixed = pl.BlockSpec((512, 512), lambda n: (0, 0))
    return pl.pallas_call(
        weight_grad_kernel,
        grid=(2,),
        in_specs=[smem] + [fixed] * 4 + [pl.BlockSpec((256, 512), lambda n: (0, n))] * 2,
        out_specs=pl.BlockSpec((4, 512, 512), lambda n: (0, 0, n)),
        out_shape=shape((4, 512, 1024)),
        compiler_params=params("arbitrary"),
        cost_estimate=pl.CostEstimate(flops=2_200_000_000, bytes_accessed=7_800_000, transcendentals=0),
        name="grad_weight",
    )(at, *columns, own, other)


def exchange(value):
    return lax.all_to_all(value, "context", split_axis=0, concat_axis=0, tiled=True)


def body(query_in, key_in, value_in, short_filter, long_filter, out_weight, grad_out):
    batches, rows, channels = query_in.shape
    scale = float(batches * rows * NCTX * GROUP) ** (-0.5)
    ctx = lax.axis_index("context")
    at_y = lax.axis_index("tensor")
    at = jnp.stack([ctx // (NC * NX), (ctx // NC) % NX, at_y, ctx % NC]).astype(jnp.int32)
    positions = batches * rows
    half = channels // 2

    taps = short_filter
    same_core = [list(range(c, NCTX, NC)) for c in range(NC)]
    weights = lax.all_gather(
        out_weight,
        "context",
        axis=0,
        tiled=True,
        axis_index_groups=same_core,
    ).reshape(NY, half, channels)
    last, mine, theirs = prep(
        at, query_in, key_in, value_in, grad_out.reshape(positions, channels)
    )
    before = next_context(last, 1)

    columns = jnp.concatenate([mine, swap_core(theirs)])
    columns, before = lax.optimization_barrier((columns, before))
    columns = around(columns, move_y)

    tiles = toeplitz_tiles(long_filter)
    prod, qf, kf, vf = featurize(taps, before, query_in, key_in, value_in)
    prod = exchange(prod)
    prod, *columns = lax.optimization_barrier((prod, *columns))
    conv = exchange(convolve(conv_kernel, "conv", prod, tiles))
    gated, conv = gate(conv, qf)
    gated_own = gated.reshape(positions, channels)
    gated_other = swap_core(gated_own)

    sums = weight_grad_call(at, columns, gated_own, gated_other).reshape(-1, channels)
    weights, sums = lax.optimization_barrier((weights, sums))
    own, other = grad_gated_call(at, columns, weights)
    other = swap_core(other)
    grad_conv, grad_gated = grad_conv_call(
        own.reshape(query_in.shape), other.reshape(query_in.shape), qf
    )
    grad_conv, gated_late = lax.optimization_barrier((grad_conv, gated_own))
    grad_conv_all = exchange(grad_conv)

    grad_weight = lax.psum_scatter(
        sums, "context", scatter_dimension=0, axis_index_groups=same_core, tiled=True
    ).astype(f32)

    mixed = mixed_call(at, gated_late, gated_other, weights)
    mixed = deliver(mixed, move_y)
    keep, send = whole(
        mixed_sum_kernel, "mixed_sum", mixed, [shape((positions, half))] * 2, index=False
    )
    (mixed_out,) = whole(
        mixed_out_kernel, "mixed_out", [at, keep, swap_core(send)], [shape((positions, channels))]
    )
    mixed_out = mixed_out.reshape(query_in.shape)
    first_q = (grad_gated[:, :HALO] * conv[:, :HALO].astype(f32)).astype(bf16)[None]
    after_q = next_context(first_q, -1)
    grad_query = grad_query_call(taps, after_q, grad_gated, conv)

    grad_product = exchange(convolve(corr_kernel, "corr", grad_conv_all, tiles))
    grad_long = grad_long_call(scale, prod, grad_conv_all)
    grad_product, grad_long, grad_query = lax.optimization_barrier(
        (grad_product, grad_long, grad_query)
    )
    grad_product, first_kv = unpack(grad_product, kf, vf)
    after_kv = next_context(first_kv, -1)
    grad_key, grad_value = grad_kv_call(taps, after_kv, grad_product, kf, vf)
    return (mixed_out, grad_query, grad_key, grad_value, grad_weight, grad_long)


def solution(mesh):
    act = P(None, "context", "tensor")
    in_specs = (
        act,
        act,
        act,
        P(None, None, "tensor"),
        P(("tensor", "context"), None),
        P("context", "tensor"),
        act,
    )
    out_specs = (act, act, act, act, P("context", "tensor"), P(("tensor", "context"), None))
    return jax.shard_map(body, mesh=mesh, in_specs=in_specs, out_specs=out_specs, check_vma=False)
```

```python
import functools

import jax
import jax.numpy as jnp
from jax import lax
from jax.experimental import pallas as pl
from jax.experimental.pallas import tpu as pltpu
from jax.sharding import PartitionSpec as P

GROUP = 16
TAPS = 7
HALO = 16
NZ, NX, NC, NY = 4, 4, 2, 4
NCTX = NZ * NX * NC
BLK = 128
CB = 256
VMEM_BYTES = 48 * 1024 * 1024
f32 = jnp.float32
bf16 = jnp.bfloat16


def move_ctx(value, dz, dx, dc):
    pairs = []
    for z in range(NZ):
        for x in range(NX):
            for c in range(NC):
                src = (z * NX + x) * NC + c
                dst = (((z + dz) % NZ) * NX + (x + dx) % NX) * NC + (c + dc) % NC
                pairs.append((src, dst))
    return lax.ppermute(value, "context", pairs)


def move_z(value, d):
    return move_ctx(value, d, 0, 0)


def move_x(value, d):
    return move_ctx(value, 0, d, 0)


def swap_core(value):
    return move_ctx(value, 0, 0, 1)


def move_y(value, d):
    return lax.ppermute(value, "tensor", [(i, (i + d) % NY) for i in range(NY)])


def next_context(value, steps):
    first, last = (max(0, -steps), min(NCTX, NCTX - steps))
    return lax.ppermute(value, "context", [(s, s + steps) for s in range(first, last)])


def around(value, move, count=4):
    return [value] + [move(value, d) for d in range(1, count)]


def deliver(parts, move):
    return [parts[0]] + [move(part, d) for d, part in enumerate(parts) if d > 0]


def params(*sem):
    return pltpu.CompilerParams(dimension_semantics=sem, vmem_limit_bytes=VMEM_BYTES)


def toeplitz_kernel(filter_ref, tile_ref):
    taps = jnp.concatenate([jnp.zeros((1, BLK), f32), filter_ref[0]], axis=1)
    blocks = taps.shape[1] // BLK - 1
    tile_ref[0, 0, BLK:, :BLK] = jnp.zeros((BLK, BLK), bf16)
    for e in range(blocks):
        window = jnp.broadcast_to(taps[:, BLK * e : BLK * (e + 2)], (BLK, 2 * BLK))
        rolled = pltpu.roll(window, 0, 1, stride=1, stride_axis=0)
        piece = rolled[:, BLK:].astype(bf16)
        if e % 2 == 0:
            tile_ref[0, e // 2, :BLK, :BLK] = piece
            tile_ref[0, e // 2, BLK:, BLK:] = piece
        else:
            tile_ref[0, e // 2, :BLK, BLK:] = piece
            if e + 1 < blocks:
                tile_ref[0, e // 2 + 1, BLK:, :BLK] = piece


def toeplitz_tiles(long_filter):
    groups, length = long_filter.shape
    tiles = length // (2 * BLK)
    return pl.pallas_call(
        toeplitz_kernel,
        grid=(groups,),
        in_specs=[pl.BlockSpec((1, 1, length), lambda g: (g, 0, 0))],
        out_specs=pl.BlockSpec((1, tiles, 2 * BLK, 2 * BLK), lambda g: (g, 0, 0, 0)),
        out_shape=jax.ShapeDtypeStruct((groups, tiles, 2 * BLK, 2 * BLK), bf16),
        compiler_params=params("arbitrary"),
        cost_estimate=pl.CostEstimate(flops=8_000_000, bytes_accessed=4_300_000, transcendentals=0),
        name="toeplitz_tiles",
    )(long_filter[:, None, :])


def spread_taps(taps_ref, stream, block):
    groups = taps_ref.shape[2]
    rows = lax.broadcasted_iota(jnp.int32, (groups, CB), 0)
    cols = lax.broadcasted_iota(jnp.int32, (groups, CB), 1)
    spread = (rows == ((block * CB + cols) >> 4)).astype(f32)
    return jnp.dot(
        taps_ref[stream], spread, precision=lax.Precision.HIGHEST, preferred_element_type=f32
    )


def to_channels(value):
    return value.T.reshape(CB // (2 * GROUP), 2, GROUP, BLK).astype(bf16)


def to_positions(value):
    return value.astype(f32).reshape(CB, BLK).T


def forward_taps(signal, halo, taps):
    ext = jnp.concatenate([halo.astype(f32), signal.astype(f32)], axis=0)
    total = taps[:1] * ext[HALO:]
    for j in range(1, TAPS):
        total = total + taps[j : j + 1] * ext[HALO - j : HALO - j + BLK]
    return total


def product_kernel(taps_ref, halo_ref, k_ref, v_ref, prod_ref, kf_ref, vf_ref):
    key_taps = spread_taps(taps_ref, 1, pl.program_id(0))
    value_taps = spread_taps(taps_ref, 2, pl.program_id(0))
    for b in range(2):
        kf_ref[b] = key = forward_taps(k_ref[b], halo_ref[1, b], key_taps)
        vf_ref[b] = value = forward_taps(v_ref[b], halo_ref[2, b], value_taps)
        prod_ref[:, :, b] = to_channels(key * value)


def query_kernel(taps_ref, halo_ref, q_ref, qf_ref):
    taps = spread_taps(taps_ref, 0, pl.program_id(0))
    for b in range(2):
        qf_ref[b] = forward_taps(q_ref[b], halo_ref[0, b], taps)


chan_spec = pl.BlockSpec((CB // (2 * GROUP), 2, 2, GROUP, BLK), lambda c: (c, 0, 0, 0, 0))
pos_spec = pl.BlockSpec((2, BLK, CB), lambda c: (0, 0, c))
taps_spec = pl.BlockSpec((3, TAPS, 64), lambda c: (0, 0, 0))
halo_spec = pl.BlockSpec((3, 2, HALO, CB), lambda c: (0, 0, 0, c))


def chan_shape():
    return jax.ShapeDtypeStruct((NCTX, 2, 2, GROUP, BLK), bf16)


def pos_shape(kind):
    return jax.ShapeDtypeStruct((2, BLK, 1024), kind)


def featurize_product(taps, halo, k, v):
    return pl.pallas_call(
        product_kernel,
        grid=(1024 // CB,),
        in_specs=[taps_spec, halo_spec, pos_spec, pos_spec],
        out_specs=[chan_spec, pos_spec, pos_spec],
        out_shape=[chan_shape(), pos_shape(f32), pos_shape(f32)],
        compiler_params=pltpu.CompilerParams(vmem_limit_bytes=62 * 1024 * 1024),
        cost_estimate=pl.CostEstimate(flops=8_000_000, bytes_accessed=3_800_000, transcendentals=0),
        name="featurize_product",
    )(taps, halo, k, v)


def featurize_query(taps, halo, q):
    return pl.pallas_call(
        query_kernel,
        grid=(1024 // CB,),
        in_specs=[taps_spec, halo_spec, pos_spec],
        out_specs=pos_spec,
        out_shape=pos_shape(f32),
        compiler_params=params("arbitrary"),
        cost_estimate=pl.CostEstimate(flops=4_000_000, bytes_accessed=1_700_000, transcendentals=0),
        name="featurize_query",
    )(taps, halo, q)


def fold(src_ref, dst_ref):
    for i in range(NCTX // 2):
        dst_ref[32 * i : 32 * i + 32, :BLK] = src_ref[2 * i, 0].reshape(32, BLK)
        dst_ref[32 * i : 32 * i + 32, BLK:] = src_ref[2 * i + 1, 0].reshape(32, BLK)


def unfold(acc_ref, dst_ref):
    for i in range(NCTX // 2):
        rows = acc_ref[32 * i : 32 * i + 32].astype(bf16)
        dst_ref[2 * i, 0] = rows[:, :BLK].reshape(2, GROUP, BLK)
        dst_ref[2 * i + 1, 0] = rows[:, BLK:].reshape(2, GROUP, BLK)


def conv_kernel(x_ref, tile_ref, out_ref, x_s, acc_s):
    fold(x_ref, x_s)
    rows = x_s.shape[0]
    for d in range(rows // 32):
        term = jnp.dot(x_s[: rows - 32 * d], tile_ref[0, d], preferred_element_type=f32)
        if d == 0:
            acc_s[...] = term
        else:
            acc_s[32 * d :] += term
    unfold(acc_s, out_ref)


def corr_kernel(x_ref, tile_ref, out_ref, x_s, acc_s):
    fold(x_ref, x_s)
    rows = x_s.shape[0]
    for d in range(rows // 32):
        term = lax.dot_general(
            x_s[32 * d :], tile_ref[0, d], (((1,), (1,)), ((), ())), preferred_element_type=f32
        )
        if d == 0:
            acc_s[...] = term
        else:
            acc_s[: rows - 32 * d] += term
    unfold(acc_s, out_ref)


group_spec = pl.BlockSpec((NCTX, 1, 2, GROUP, BLK), lambda g: (0, g, 0, 0, 0))
tile_spec = pl.BlockSpec((1, 16, 2 * BLK, 2 * BLK), lambda g: (g, 0, 0, 0))


def convolve(kernel, name, x, tiles):
    return pl.pallas_call(
        kernel,
        grid=(2,),
        in_specs=[group_spec, tile_spec],
        out_specs=group_spec,
        out_shape=chan_shape(),
        scratch_shapes=[pltpu.VMEM((512, 256), bf16), pltpu.VMEM((512, 256), f32)],
        compiler_params=params("arbitrary"),
        cost_estimate=pl.CostEstimate(flops=1_100_000_000, bytes_accessed=5_300_000, transcendentals=0),
        name=name,
    )(x, tiles)


def grad_long_kernel(scale, p_ref, g_ref, out_ref, p_s, g_s):
    fold(p_ref, p_s)
    fold(g_ref, g_s)
    g_s[512:] = jnp.zeros((512, 256), bf16)
    rows = lax.broadcasted_iota(jnp.int32, (256, 256), 0)
    cols = lax.broadcasted_iota(jnp.int32, (256, 256), 1)
    flip = (rows + cols == 255).astype(bf16)
    back = lax.dot_general(
        flip, p_s[...], (((1,), (1,)), ((), ())), preferred_element_type=f32
    ).astype(bf16)

    def diagonals(block):
        padded = jnp.concatenate([block, jnp.zeros((BLK, BLK), f32)], axis=1)
        rolled = pltpu.roll(padded, 1, 1, stride=1, stride_axis=0)
        return jnp.sum(rolled, axis=0, keepdims=True)

    def gram(d):
        return jnp.dot(back, g_s[32 * d : 32 * d + 512], preferred_element_type=f32)

    here = gram(0)
    lag = diagonals(here[BLK:, :BLK] + here[:BLK, BLK:])
    for d in range(16):
        later = gram(d + 1) if d < 15 else None
        cross = here[BLK:, BLK:]
        if later is not None:
            cross = cross + later[:BLK, :BLK]
        odd = diagonals(cross)
        out_ref[0, :, 256 * d : 256 * d + BLK] = scale * (lag[:, BLK:] + odd[:, :BLK])
        if later is not None:
            lag = diagonals(later[BLK:, :BLK] + later[:BLK, BLK:])
            out_ref[0, :, 256 * d + BLK : 256 * d + 256] = scale * (odd[:, BLK:] + lag[:, :BLK])
        else:
            out_ref[0, :, 256 * d + BLK : 256 * d + 256] = scale * odd[:, BLK:]
        here = later


def grad_long_call(scale, prod, grad_conv):
    return pl.pallas_call(
        functools.partial(grad_long_kernel, scale),
        grid=(2,),
        in_specs=[group_spec, group_spec],
        out_specs=pl.BlockSpec((1, 1, NCTX * BLK), lambda g: (g, 0, 0)),
        out_shape=jax.ShapeDtypeStruct((2, 1, NCTX * BLK), f32),
        scratch_shapes=[pltpu.VMEM((512, 256), bf16), pltpu.VMEM((1024, 256), bf16)],
        compiler_params=params("arbitrary"),
        cost_estimate=pl.CostEstimate(flops=2_200_000_000, bytes_accessed=1_200_000, transcendentals=0),
        name="grad_long",
    )(prod, grad_conv)[:, 0]


def gate_kernel(conv_ref, qf_ref, gated_ref, convp_ref):
    for b in range(2):
        conv = to_positions(conv_ref[:, :, b])
        convp_ref[b] = conv.astype(bf16)
        gated_ref[b] = (qf_ref[b] * conv).astype(bf16)


def gate(conv, qf):
    return pl.pallas_call(
        gate_kernel,
        grid=(1024 // CB,),
        in_specs=[chan_spec, pos_spec],
        out_specs=[pos_spec, pos_spec],
        out_shape=[pos_shape(bf16), pos_shape(bf16)],
        compiler_params=params("arbitrary"),
        cost_estimate=pl.CostEstimate(flops=1_000_000, bytes_accessed=2_500_000, transcendentals=0),
        name="gate",
    )(conv, qf)


def grad_conv_kernel(own_ref, other_ref, qf_ref, gc_ref, gg_ref):
    for b in range(2):
        total = own_ref[b] + other_ref[b].astype(f32)
        gg_ref[b] = total
        gc_ref[:, :, b] = to_channels(total * qf_ref[b])


def grad_conv_call(own, other, qf):
    return pl.pallas_call(
        grad_conv_kernel,
        grid=(1024 // CB,),
        in_specs=[pos_spec, pos_spec, pos_spec],
        out_specs=[chan_spec, pos_spec],
        out_shape=[chan_shape(), pos_shape(f32)],
        compiler_params=params("arbitrary"),
        cost_estimate=pl.CostEstimate(flops=1_000_000, bytes_accessed=4_000_000, transcendentals=0),
        name="grad_conv",
    )(own, other, qf)


def unpack_kernel(gp_ref, kf_ref, vf_ref, gpp_ref, first_ref):
    for b in range(2):
        grad = to_positions(gp_ref[:, :, b])
        gpp_ref[b] = grad.astype(bf16)
        first_ref[0, b] = (grad[:HALO] * vf_ref[b]).astype(bf16)
        first_ref[1, b] = (grad[:HALO] * kf_ref[b]).astype(bf16)


def unpack(gp, kf, vf):
    rows_spec = pl.BlockSpec((2, HALO, CB), lambda c: (0, 0, c))
    return pl.pallas_call(
        unpack_kernel,
        grid=(1024 // CB,),
        in_specs=[chan_spec, rows_spec, rows_spec],
        out_specs=[pos_spec, pl.BlockSpec((2, 2, HALO, CB), lambda c: (0, 0, 0, c))],
        out_shape=[pos_shape(bf16), jax.ShapeDtypeStruct((2, 2, HALO, 1024), bf16)],
        compiler_params=params("arbitrary"),
        cost_estimate=pl.CostEstimate(flops=500_000, bytes_accessed=1_200_000, transcendentals=0),
        name="unpack",
    )(gp, kf, vf)


def backward_taps(grad, halo, taps):
    ext = jnp.concatenate([grad, halo.astype(f32)], axis=0)
    total = taps[:1] * grad
    for j in range(1, TAPS):
        total = total + taps[j : j + 1] * ext[j : j + BLK]
    return total.astype(bf16)


def grad_query_kernel(taps_ref, halo_ref, gg_ref, conv_ref, out_ref):
    taps = spread_taps(taps_ref, 0, pl.program_id(0))
    for b in range(2):
        out_ref[b] = backward_taps(gg_ref[b] * conv_ref[b].astype(f32), halo_ref[0, b], taps)


def grad_query_call(taps, halo, gg, conv):
    return pl.pallas_call(
        grad_query_kernel,
        grid=(1024 // CB,),
        in_specs=[
            taps_spec,
            pl.BlockSpec((1, 2, HALO, CB), lambda c: (0, 0, 0, c)),
            pos_spec,
            pos_spec,
        ],
        out_specs=pos_spec,
        out_shape=pos_shape(bf16),
        compiler_params=params("arbitrary"),
        cost_estimate=pl.CostEstimate(flops=4_000_000, bytes_accessed=2_100_000, transcendentals=0),
        name="grad_query",
    )(taps, halo, gg, conv)


def grad_kv_kernel(taps_ref, halo_ref, gp_ref, kf_ref, vf_ref, gk_ref, gv_ref):
    key_taps = spread_taps(taps_ref, 1, pl.program_id(0))
    value_taps = spread_taps(taps_ref, 2, pl.program_id(0))
    for b in range(2):
        grad = gp_ref[b].astype(f32)
        gk_ref[b] = backward_taps(grad * vf_ref[b], halo_ref[0, b], key_taps)
        gv_ref[b] = backward_taps(grad * kf_ref[b], halo_ref[1, b], value_taps)


def grad_kv_call(taps, halo, gp, kf, vf):
    return pl.pallas_call(
        grad_kv_kernel,
        grid=(1024 // CB,),
        in_specs=[
            taps_spec,
            pl.BlockSpec((2, 2, HALO, CB), lambda c: (0, 0, 0, c)),
            pos_spec,
            pos_spec,
            pos_spec,
        ],
        out_specs=[pos_spec, pos_spec],
        out_shape=[pos_shape(bf16), pos_shape(bf16)],
        compiler_params=params("arbitrary"),
        cost_estimate=pl.CostEstimate(flops=8_000_000, bytes_accessed=4_000_000, transcendentals=0),
        name="grad_kv",
    )(taps, halo, gp, kf, vf)


def vmem(count=1):
    return [pl.BlockSpec(memory_space=pltpu.VMEM)] * count


smem = pl.BlockSpec(memory_space=pltpu.SMEM)


def whole(kernel, name, ins, outs, flops=0, scratch=(), index=True):
    size = sum(a.size * a.dtype.itemsize for a in ins)
    size += sum(a.size * jnp.dtype(a.dtype).itemsize for a in outs)
    return pl.pallas_call(
        kernel,
        in_specs=([smem] if index else []) + vmem(len(ins) - int(index)),
        out_specs=vmem(len(outs)),
        out_shape=list(outs),
        scratch_shapes=list(scratch),
        compiler_params=pltpu.CompilerParams(vmem_limit_bytes=VMEM_BYTES),
        cost_estimate=pl.CostEstimate(flops=flops, bytes_accessed=size, transcendentals=0),
        name=name,
    )(*ins)


def shape(dims, kind=bf16):
    return jax.ShapeDtypeStruct(dims, kind)


def prep_kernel(at, q_ref, k_ref, v_ref, g_ref, last_ref, mine_ref, theirs_ref):
    first_core = at[3] == 0
    for i, src in enumerate((q_ref, k_ref, v_ref)):
        last_ref[i] = src[...]
    for x in range(NX):
        lo = g_ref[:, 256 * x : 256 * x + BLK]
        hi = g_ref[:, 256 * x + BLK : 256 * x + 256]
        mine_ref[:, BLK * x : BLK * x + BLK] = jnp.where(first_core, lo, hi)
        theirs_ref[:, BLK * x : BLK * x + BLK] = jnp.where(first_core, hi, lo)


def prep(at, q, k, v, grad_out):
    rows = pl.BlockSpec((2, HALO, 1024), lambda i: (0, BLK // HALO - 1, 0))
    full = lambda dims: pl.BlockSpec(dims, lambda i: (0,) * len(dims))
    return pl.pallas_call(
        prep_kernel,
        grid=(1,),
        in_specs=[smem, rows, rows, rows, full((256, 1024))],
        out_specs=[full((3, 2, HALO, 1024)), full((256, 512)), full((256, 512))],
        out_shape=[
            shape((3, 2, HALO, 1024)),
            shape((256, 512)),
            shape((256, 512)),
        ],
        compiler_params=pltpu.CompilerParams(vmem_limit_bytes=62 * 1024 * 1024),
        name="prep",
    )(at, q, k, v, grad_out)


def grad_gated_kernel(at, c0, c1, c2, c3, w_ref, own_ref, other_ref):
    total = jnp.zeros((512, 256), f32)
    for d, cols in enumerate((c0, c1, c2, c3)):
        total = total + jnp.dot(
            cols[...], w_ref[(at[2] + 4 - d) & 3], preferred_element_type=f32
        )
    own_ref[...] = total[:256]
    other_ref[...] = total[256:].astype(bf16)


def grad_gated_call(at, columns, weights):
    fixed = pl.BlockSpec((512, 512), lambda n: (0, 0))
    return pl.pallas_call(
        grad_gated_kernel,
        grid=(4,),
        in_specs=[smem] + [fixed] * 4 + [pl.BlockSpec((4, 512, 256), lambda n: (0, 0, n))],
        out_specs=[pl.BlockSpec((256, 256), lambda n: (0, n))] * 2,
        out_shape=[shape((256, 1024), f32), shape((256, 1024))],
        compiler_params=params("arbitrary"),
        cost_estimate=pl.CostEstimate(flops=2_200_000_000, bytes_accessed=7_800_000, transcendentals=0),
        name="grad_gated",
    )(at, *columns, weights)


def mixed_kernel(at, own_g, other_g, w_ref, *outs):
    for d in range(4):
        block = w_ref[(at[2] + d) & 3]
        for i, src in enumerate((own_g, other_g)):
            part = lax.dot_general(
                src[...], block, (((1,), (1,)), ((), ())), preferred_element_type=f32
            )
            outs[d][256 * i : 256 * i + 256] = part.astype(outs[d].dtype)


def mixed_call(at, own, other, weights):
    fixed = pl.BlockSpec((256, 1024), lambda n: (0, 0))
    return pl.pallas_call(
        mixed_kernel,
        grid=(2,),
        in_specs=[smem, fixed, fixed, pl.BlockSpec((4, 256, 1024), lambda n: (0, n, 0))],
        out_specs=[pl.BlockSpec((512, 256), lambda n: (0, n))] * 4,
        out_shape=[shape((512, 512), f32)] + [shape((512, 512))] * 3,
        compiler_params=params("arbitrary"),
        cost_estimate=pl.CostEstimate(flops=2_200_000_000, bytes_accessed=7_800_000, transcendentals=0),
        name="mixed",
    )(at, own, other, weights)


def mixed_sum_kernel(own, a_ref, b_ref, c_ref, keep_ref, send_ref):
    total = own[...] + a_ref[...].astype(f32) + b_ref[...].astype(f32) + c_ref[...].astype(f32)
    keep_ref[...] = total[:256].astype(bf16)
    send_ref[...] = total[256:].astype(bf16)


def mixed_out_kernel(at, keep_ref, came_ref, out_ref):
    first_core = at[3] == 0
    for x in range(NX):
        keep = keep_ref[:, BLK * x : BLK * x + BLK]
        came = came_ref[:, BLK * x : BLK * x + BLK]
        out_ref[:, 256 * x : 256 * x + BLK] = jnp.where(first_core, keep, came)
        out_ref[:, 256 * x + BLK : 256 * x + 256] = jnp.where(first_core, came, keep)


def weight_grad_kernel(at, c0, c1, c2, c3, own_g, other_g, out_ref):
    for d, cols in enumerate((c0, c1, c2, c3)):
        total = 0.0
        for i, src in enumerate((own_g, other_g)):
            total = total + lax.dot_general(
                cols[256 * i : 256 * i + 256],
                src[...],
                (((0,), (0,)), ((), ())),
                preferred_element_type=f32,
            )
        out_ref[(at[2] + 4 - d) & 3] = total.astype(bf16)


def weight_grad_call(at, columns, own, other):
    fixed = pl.BlockSpec((512, 512), lambda n: (0, 0))
    return pl.pallas_call(
        weight_grad_kernel,
        grid=(2,),
        in_specs=[smem] + [fixed] * 4 + [pl.BlockSpec((256, 512), lambda n: (0, n))] * 2,
        out_specs=pl.BlockSpec((4, 512, 512), lambda n: (0, 0, n)),
        out_shape=shape((4, 512, 1024)),
        compiler_params=pltpu.CompilerParams(vmem_limit_bytes=62 * 1024 * 1024),
        cost_estimate=pl.CostEstimate(flops=2_200_000_000, bytes_accessed=7_800_000, transcendentals=0),
        name="grad_weight",
    )(at, *columns, own, other)


def exchange(value):
    return lax.all_to_all(value, "context", split_axis=0, concat_axis=0, tiled=True)


def body(query_in, key_in, value_in, short_filter, long_filter, out_weight, grad_out):
    batches, rows, channels = query_in.shape
    scale = float(batches * rows * NCTX * GROUP) ** (-0.5)
    ctx = lax.axis_index("context")
    at_y = lax.axis_index("tensor")
    at = jnp.stack([ctx // (NC * NX), (ctx // NC) % NX, at_y, ctx % NC]).astype(jnp.int32)
    positions = batches * rows
    half = channels // 2

    taps = short_filter
    same_core = [list(range(c, NCTX, NC)) for c in range(NC)]
    weights = lax.all_gather(
        out_weight,
        "context",
        axis=0,
        tiled=True,
        axis_index_groups=same_core,
    ).reshape(NY, half, channels)
    last, mine, theirs = prep(
        at, query_in, key_in, value_in, grad_out.reshape(positions, channels)
    )
    before = next_context(last, 1)

    columns = jnp.concatenate([mine, swap_core(theirs)])
    columns, before = lax.optimization_barrier((columns, before))
    columns = around(columns, move_y)

    tiles = toeplitz_tiles(long_filter)
    prod, kf, vf = featurize_product(taps, before, key_in, value_in)
    prod = exchange(prod)
    prod, *columns = lax.optimization_barrier((prod, *columns))
    conv = convolve(conv_kernel, "conv", prod, tiles)
    conv, before = lax.optimization_barrier((conv, before))
    conv = exchange(conv)
    qf = featurize_query(taps, before, query_in)
    gated, conv = gate(conv, qf)
    gated_own = gated.reshape(positions, channels)
    gated_other = swap_core(gated_own)

    sums = weight_grad_call(at, columns, gated_own, gated_other).reshape(-1, channels)
    weights, sums = lax.optimization_barrier((weights, sums))
    own, other = grad_gated_call(at, columns, weights)
    other = swap_core(other)
    grad_conv, grad_gated = grad_conv_call(
        own.reshape(query_in.shape), other.reshape(query_in.shape), qf
    )
    grad_conv, gated_late = lax.optimization_barrier((grad_conv, gated_own))
    grad_conv_all = exchange(grad_conv)

    grad_weight = lax.psum_scatter(
        sums, "context", scatter_dimension=0, axis_index_groups=same_core, tiled=True
    ).astype(f32)

    mixed = mixed_call(at, gated_late, gated_other, weights)
    mixed = deliver(mixed, move_y)
    keep, send = whole(
        mixed_sum_kernel, "mixed_sum", mixed, [shape((positions, half))] * 2, index=False
    )
    (mixed_out,) = whole(
        mixed_out_kernel, "mixed_out", [at, keep, swap_core(send)], [shape((positions, channels))]
    )
    mixed_out = mixed_out.reshape(query_in.shape)
    first_q = (grad_gated[:, :HALO] * conv[:, :HALO].astype(f32)).astype(bf16)[None]
    after_q = next_context(first_q, -1)
    grad_query = grad_query_call(taps, after_q, grad_gated, conv)

    grad_product = exchange(convolve(corr_kernel, "corr", grad_conv_all, tiles))
    grad_long = grad_long_call(scale, prod, grad_conv_all)
    grad_product, grad_long, grad_query = lax.optimization_barrier(
        (grad_product, grad_long, grad_query)
    )
    grad_product, first_kv = unpack(grad_product, kf, vf)
    after_kv = next_context(first_kv, -1)
    grad_key, grad_value = grad_kv_call(taps, after_kv, grad_product, kf, vf)
    return (mixed_out, grad_query, grad_key, grad_value, grad_weight, grad_long)


def solution(mesh):
    act = P(None, "context", "tensor")
    in_specs = (
        act,
        act,
        act,
        P(None, None, "tensor"),
        P(("tensor", "context"), None),
        P("context", "tensor"),
        act,
    )
    out_specs = (act, act, act, act, P("context", "tensor"), P(("tensor", "context"), None))
    return jax.shard_map(body, mesh=mesh, in_specs=in_specs, out_specs=out_specs, check_vma=False)
```
